128 devices in a mesh: band: 8 (over z_lo, y), grid: 16 (over x, z_hi, core).
Axes of the slice: x: 4, y: 4, z: 4 (z_hi: 2, z_lo: 2; z = z_hi * 2 + z_lo), core: 2. Of those that a mesh axis runs over, the one named last changes fastest.
Arguments:
- basis: float32 [128, 2, 1024, 128], P('band', None, 'grid'), may hold values from -6 to 6
- rotation: float32 [128, 16], replicated, may hold values from -0.5 to 0.5
- ritz_values: float32 [16], P('band'), may hold values from -1 to 3
- potential: float32 [128, 128, 128], P('grid'), may hold values from -4 to 4
- col_map: int32 [1024], replicated, may hold values from 0 to 16383, as said below
Outputs:
- resid: float32 [16, 2, 1024, 128], P('band', None, 'grid')
- h_resid: float32 [16, 2, 1024, 128], P('band', None, 'grid')
- intersection: float32 [128, 16], P('band')
The draws below stay inside these ranges and needn't reach their ends.
Inputs may be any that keep to these rules, and one draw needn't show every extreme that they name: `col_map`: the 1024 positions are distinct.
All inputs are finite; a program needn't handle non-finite values.
Results may differ from the reference program's by a relative error of at most 0.0003.
Values sent between devices are 32-bit elements; how exact they have to be, the bound alone decides.
A program may use at most 64 MiB of HBM per device.

```python
import jax
import jax.numpy as jnp
from jax import lax

N = 128
NB = 16
NS = 128
NCOL = 1024


def draw_col_map(key, part):
    key = jax.random.fold_in(key, 7)
    first_key, second_key = jax.random.split(key)
    inner = jax.random.permutation(first_key, N * N - 2)[:NCOL - 2].astype(jnp.int32) + 1
    whole = jnp.concatenate([jnp.zeros((1,), jnp.int32), inner, jnp.full((1,), N * N - 1, jnp.int32)])
    order = jax.random.permutation(second_key, NCOL)
    return whole[order].astype(jnp.int32)


def block_levels(own_key, dims, pieces, low, largest):
    factor_of = 1.0
    for dim, parts in pieces:
        steps = jax.random.uniform(jax.random.fold_in(jax.random.fold_in(own_key, 6), dim), (parts,), jnp.float32, low / len(pieces), largest / len(pieces))
        factor_of = factor_of * jnp.repeat(jnp.exp(steps), dims[dim] // parts).reshape((-1,) + (1,) * (len(dims) - 1 - dim))
    return factor_of


def noise(key, extent, deviation, limit, cuts=(), kind=jnp.bfloat16):
    values = deviation * jax.random.normal(key, extent, jnp.float32)
    if cuts:
        values = values * block_levels(key, extent, cuts, -0.22, 0.18)
    return jnp.clip(values, -limit, limit).astype(kind)


def setup_inputs(seed: int = 0) -> dict:
    arg_keys = jax.random.split(jax.random.key(seed), 6)
    basis = noise(arg_keys[0], (NS, 2, NCOL, N), 1.0, 6.0, ((0, 8), (2, 16)), jnp.float32)
    rotation = noise(arg_keys[1], (NS, NB), NS ** -0.5, 0.5, (), jnp.float32)
    ritz_values = jnp.clip(-1.0 + 4.0 * jax.random.uniform(arg_keys[2], (NB,), jnp.float32) ** block_levels(arg_keys[2], (NB,), ((0, 8),), -0.2, 0.2), -1.0, 3.0)
    potential = noise(arg_keys[3], (N, N, N), 1.0, 4.0, ((0, 16),), jnp.float32)
    col_map = draw_col_map(jax.random.fold_in(arg_keys[5], 71), 0)
    return dict(basis=basis, rotation=rotation, ritz_values=ritz_values, potential=potential, col_map=col_map)


kinetic_coef = 2.0


def frequencies(values):
    return jnp.where(values >= N // 2, values - N, values)


def kinetic_table(positions):
    x_freq = frequencies(positions // N)
    y_freq = frequencies(positions % N)
    z_freq = frequencies(jnp.arange(N, dtype=jnp.int32))
    summed = (x_freq * x_freq + y_freq * y_freq)[:, None] + (z_freq * z_freq)[None, :]
    return kinetic_coef * summed.astype(jnp.float32) / float((N // 2) ** 2)


def apply_band(pair, potential_xyz, x_index, y_index, kinetic):
    values = lax.complex(pair[0], pair[1])
    full_grid = jnp.zeros((N, N, N), values.dtype).at[x_index, y_index].set(values)
    field = jnp.fft.ifftn(full_grid) * potential_xyz
    back = jnp.fft.fftn(field)[x_index, y_index]
    return jnp.stack([jnp.real(back), jnp.imag(back)]) + kinetic[None] * pair


def apply_hamiltonian(coeffs, potential, positions, kinetic):
    potential_xyz = jnp.transpose(potential, (1, 2, 0))
    x_index = positions // N
    y_index = positions % N
    return lax.map(lambda pair: apply_band(pair, potential_xyz, x_index, y_index, kinetic), coeffs)


def reference(basis, rotation, ritz_values, potential, col_map):
    kinetic = kinetic_table(col_map)
    ritz = jnp.einsum("ij,ipcz->jpcz", rotation, basis, precision=lax.Precision.HIGHEST)
    image = apply_hamiltonian(ritz, potential, col_map, kinetic)
    resid = (image - ritz_values[:, None, None, None] * ritz) / (1.0 + kinetic)
    h_resid = apply_hamiltonian(resid, potential, col_map, kinetic)
    intersection = jnp.einsum("ipcz,jpcz->ij", basis, resid, precision=lax.Precision.HIGHEST) / float(2 * N * NCOL)
    return resid, h_resid, intersection
```

```python
import functools

import jax
import jax.numpy as jnp
import ml_dtypes
import numpy as np
from jax import lax
from jax.experimental import pallas as pl
from jax.experimental.pallas import tpu as pltpu
from jax.sharding import PartitionSpec as P

MESH = pl.DeviceIdType.MESH
N = 128
HALF = 64
LOW = 32
TOP = N // LOW
KINETIC_COEF = 2.0
F32 = jnp.float32
BF16 = jnp.bfloat16


def angle_tables():
    index = np.arange(N)
    angles = 2.0 * np.pi * (np.outer(index, index) % N) / N
    return np.cos(angles), np.sin(angles)


def split_table(table):
    high = table.astype(ml_dtypes.bfloat16)
    low = (table - high.astype(np.float64)).astype(ml_dtypes.bfloat16)
    return np.stack([high, low])


def make_tables():
    cosine, sine = angle_tables()
    inverse_z = (np.concatenate([cosine, sine], axis=1) / N).astype(np.float32)
    forward_z = np.concatenate([cosine, sine], axis=0).astype(np.float32)
    inverse = np.block([[cosine, sine], [-sine, cosine]]) / N
    forward = np.block([[cosine, -sine], [sine, cosine]])
    tables = np.concatenate(
        [split_table(inverse), split_table(inverse.T), split_table(forward), split_table(forward.T)]
    )
    return inverse_z, forward_z, tables


RIGHT_INV, LEFT_INV, RIGHT_FWD, LEFT_FWD = 0, 2, 4, 6


def split(value):
    high = value.astype(BF16)
    return high, (value - high.astype(F32)).astype(BF16)


def dot(left, right):
    return jnp.dot(left, right, preferred_element_type=F32)


def wait_bytes(view, sem):
    pltpu.make_async_copy(view, view, sem).wait()


def kernel(
    n_band, n_grid, total,
    basis_ref, rot_ref, ritz_val_ref, pot_ref, map_ref, tzi_ref, tzf_ref, tab_ref,
    resid_ref, hres_ref, inter_ref,
    part, rs, coeff, kin, onehot, onehot_t, mask, tmp,
    send_f, recv_f, send_b, recv_b,
    vals, wide_h, wide_l, rows_h, rows_l, cols_h, cols_l, read_h, read_l,
    gath, acc, psend, precv,
    rs_send, rs_recv, f_send, f_recv, b_send, b_recv, g_send, g_recv, p_send, p_recv,
):
    slabs = N // n_grid
    chunks = total // N
    n_sub = basis_ref.shape[0]
    my_band = lax.axis_index("band")
    my_grid = lax.axis_index("grid")

    barrier = pltpu.get_barrier_semaphore()

    def greet_band(step, carry):
        peer = lax.rem(my_band + step, n_band)
        pl.semaphore_signal(barrier, inc=1, device_id=(peer, my_grid), device_id_type=MESH)
        return carry

    def greet_grid(step, carry):
        peer = lax.rem(my_grid + step, n_grid)
        pl.semaphore_signal(barrier, inc=1, device_id=(my_band, peer), device_id_type=MESH)
        return carry

    lax.fori_loop(1, n_band, greet_band, 0)
    lax.fori_loop(1, n_grid, greet_grid, 0)
    pl.semaphore_wait(barrier, n_band - 1 + n_grid - 1)

    def partial_of(owner, which):
        column = owner * 2 + which
        row = my_band * n_sub
        value = rot_ref[row, column] * basis_ref[0]
        for i in range(1, n_sub):
            value = value + rot_ref[row + i, column] * basis_ref[i]
        return value

    for which in range(2):
        def send_partial(step, carry, which=which):
            owner = lax.rem(my_band + step, n_band)
            part[which, owner] = partial_of(owner, which)
            pltpu.make_async_remote_copy(
                src_ref=part.at[which, owner],
                dst_ref=rs.at[which, my_band],
                send_sem=rs_send.at[which],
                recv_sem=rs_recv.at[which],
                device_id=(owner, my_grid),
                device_id_type=MESH,
            ).start()
            return carry

        lax.fori_loop(1, n_band, send_partial, 0)
        rs[which, my_band] = partial_of(my_band, which)

    lane_c = lax.broadcasted_iota(jnp.int32, (TOP * N, N), 0)
    lane_r = lax.broadcasted_iota(jnp.int32, (LOW, N), 0)
    for j in range(chunks):
        span = slice(j * N, (j + 1) * N)
        pos = map_ref[j:j + 1, :]
        x = lax.shift_right_logical(pos, 7)
        y = lax.bitwise_and(pos, N - 1)
        high = lax.shift_right_logical(x, 5) * N + y
        hit = jnp.where(lane_c == jnp.broadcast_to(high, lane_c.shape), 1.0, 0.0)
        onehot_t[:, span] = hit.astype(BF16)
        for t in range(TOP):
            onehot[span, t * N:(t + 1) * N] = hit[t * N:(t + 1) * N].T.astype(BF16)
        low = jnp.broadcast_to(lax.bitwise_and(x, LOW - 1), lane_r.shape)
        mask[:, span] = jnp.where(lane_r == low, 1.0, 0.0)

    mine = map_ref[pl.ds(my_grid // 2, 1), :].astype(F32)
    tmp[...] = jnp.broadcast_to(mine, (N, N)).T
    here = tmp[pl.ds(pl.multiple_of(lax.rem(my_grid, 2) * HALF, HALF), HALF), :].astype(jnp.int32)
    fx = lax.shift_right_logical(here, 7)
    fy = lax.bitwise_and(here, N - 1)
    fz = lax.broadcasted_iota(jnp.int32, (HALF, N), 1)
    fx = jnp.where(fx >= HALF, fx - N, fx)
    fy = jnp.where(fy >= HALF, fy - N, fy)
    fz = jnp.where(fz >= HALF, fz - N, fz)
    squares = (fx * fx + fy * fy + fz * fz).astype(F32)
    kinetic = squares * (KINETIC_COEF / float((N // 2) ** 2))
    kin[0:HALF] = kinetic
    kin[HALF:N] = kinetic

    lane = lax.broadcasted_iota(jnp.int32, (slabs, N), 1)
    first = lane < HALF

    def exchange(send, recv, send_sem, recv_sem, unit):
        def go(step, carry):
            peer = lax.rem(my_grid + step, n_grid)
            there = pl.multiple_of(peer * slabs, slabs)
            here_at = pl.multiple_of(my_grid * slabs, slabs)
            pltpu.make_async_remote_copy(
                src_ref=send.at[unit, pl.ds(there, slabs)],
                dst_ref=recv.at[unit, pl.ds(here_at, slabs)],
                send_sem=send_sem.at[unit],
                recv_sem=recv_sem.at[unit],
                device_id=(my_band, peer),
                device_id_type=MESH,
            ).start()
            return carry

        lax.fori_loop(1, n_grid, go, 0)
        own = pl.multiple_of(my_grid * slabs, slabs)
        recv[unit, pl.ds(own, slabs)] = send[unit, pl.ds(own, slabs)]

    def wait_exchange(recv, sem, unit):
        wait_bytes(recv.at[unit, pl.ds(0, N - slabs)], sem.at[unit])

    def spread(value, unit):
        real, imag = value[0:HALF], value[HALF:N]
        right = jnp.concatenate(
            [jnp.concatenate([real, -imag], axis=1), jnp.concatenate([imag, real], axis=1)], axis=0
        )
        send_f[unit] = lax.dot_general(
            tzi_ref[...], right, (((1,), (1,)), ((), ())),
            precision=lax.Precision.HIGHEST, preferred_element_type=F32,
        )
        exchange(send_f, recv_f, f_send, f_recv, unit)

    def ritz_ready(which):
        wait_bytes(rs.at[which, pl.ds(0, n_band - 1)], rs_recv.at[which])
        value = rs[which, 0]
        for d in range(1, n_band):
            value = value + rs[which, d]
        coeff[which] = value
        spread(value, which)

    def plane_inverse(unit):
        wait_exchange(recv_f, f_recv, unit)
        for j in range(chunks):
            span = slice(j * N, (j + 1) * N)
            left = recv_f[unit, 2 * j * slabs:(2 * j + 1) * slabs]
            right = recv_f[unit, (2 * j + 1) * slabs:(2 * j + 2) * slabs]
            vals[0:slabs, span] = jnp.where(first, left, pltpu.roll(right, HALF, 1))
            vals[slabs:2 * slabs, span] = jnp.where(first, pltpu.roll(left, HALF, 1), right)
        chosen = mask[...] > 0.5
        for k in range(2 * slabs):
            row = vals[k:k + 1, :]
            high = row.astype(BF16).astype(F32)
            low = row - high
            span = slice(k * LOW, (k + 1) * LOW)
            wide_h[span] = jnp.where(chosen, jnp.broadcast_to(high, chosen.shape), 0.0).astype(BF16)
            wide_l[span] = jnp.where(chosen, jnp.broadcast_to(low, chosen.shape), 0.0).astype(BF16)
        for wide, rows in ((wide_h, rows_h), (wide_l, rows_l)):
            placed = dot(wide[...], onehot[...]).astype(BF16)
            for q in range(2):
                for s in range(slabs):
                    k = q * slabs + s
                    for t in range(TOP):
                        rows[s * N + t * LOW:s * N + (t + 1) * LOW, q * N:(q + 1) * N] = placed[
                            k * LOW:(k + 1) * LOW, t * N:(t + 1) * N
                        ]
        along_y = (
            dot(rows_h[...], tab_ref[RIGHT_INV])
            + dot(rows_h[...], tab_ref[RIGHT_INV + 1])
            + dot(rows_l[...], tab_ref[RIGHT_INV])
        )
        high, low = split(along_y)
        for q in range(2):
            for s in range(slabs):
                cols_h[q * N:(q + 1) * N, s * N:(s + 1) * N] = high[s * N:(s + 1) * N, q * N:(q + 1) * N]
                cols_l[q * N:(q + 1) * N, s * N:(s + 1) * N] = low[s * N:(s + 1) * N, q * N:(q + 1) * N]
        field = (
            dot(tab_ref[LEFT_INV], cols_h[...])
            + dot(tab_ref[LEFT_INV + 1], cols_h[...])
            + dot(tab_ref[LEFT_INV], cols_l[...])
        )
        for s in range(slabs):
            span = slice(s * N, (s + 1) * N)
            here_pot = pot_ref[s]
            for q in range(2):
                high, low = split(field[q * N:(q + 1) * N, span] * here_pot)
                cols_h[q * N:(q + 1) * N, span] = high
                cols_l[q * N:(q + 1) * N, span] = low

    def plane_forward(unit):
        along_x = (
            dot(tab_ref[LEFT_FWD], cols_h[...])
            + dot(tab_ref[LEFT_FWD + 1], cols_h[...])
            + dot(tab_ref[LEFT_FWD], cols_l[...])
        )
        high, low = split(along_x)
        for q in range(2):
            for s in range(slabs):
                rows_h[s * N:(s + 1) * N, q * N:(q + 1) * N] = high[q * N:(q + 1) * N, s * N:(s + 1) * N]
                rows_l[s * N:(s + 1) * N, q * N:(q + 1) * N] = low[q * N:(q + 1) * N, s * N:(s + 1) * N]
        along_y = (
            dot(rows_h[...], tab_ref[RIGHT_FWD])
            + dot(rows_h[...], tab_ref[RIGHT_FWD + 1])
            + dot(rows_l[...], tab_ref[RIGHT_FWD])
        )
        high, low = split(along_y)
        for q in range(2):
            for s in range(slabs):
                k = q * slabs + s
                for t in range(TOP):
                    at = slice(s * N + t * LOW, s * N + (t + 1) * LOW)
                    read_h[k * LOW:(k + 1) * LOW, t * N:(t + 1) * N] = high[at, q * N:(q + 1) * N]
                    read_l[k * LOW:(k + 1) * LOW, t * N:(t + 1) * N] = low[at, q * N:(q + 1) * N]
        picked = dot(read_h[...], onehot_t[...]) + dot(read_l[...], onehot_t[...])
        for k in range(2 * slabs):
            vals[k:k + 1, :] = jnp.sum(
                picked[k * LOW:(k + 1) * LOW] * mask[...], axis=0, keepdims=True
            )
        for j in range(chunks):
            span = slice(j * N, (j + 1) * N)
            real = vals[0:slabs, span]
            imag = vals[slabs:2 * slabs, span]
            send_b[unit, 2 * j * slabs:(2 * j + 1) * slabs] = jnp.where(
                first, real, pltpu.roll(imag, HALF, 1)
            )
            send_b[unit, (2 * j + 1) * slabs:(2 * j + 2) * slabs] = jnp.where(
                first, pltpu.roll(real, HALF, 1), imag
            )
        exchange(send_b, recv_b, b_send, b_recv, unit)

    def finish(unit, which):
        wait_exchange(recv_b, b_recv, unit)
        turned = recv_b[unit].T
        real, imag = turned[0:HALF], turned[HALF:N]
        left = jnp.concatenate(
            [jnp.concatenate([real, imag], axis=1), jnp.concatenate([imag, -real], axis=1)], axis=0
        )
        value = jnp.dot(
            left, tzf_ref[...], precision=lax.Precision.HIGHEST, preferred_element_type=F32
        )
        return value + kin[...] * coeff[which]

    def residual(unit):
        which = unit
        image = finish(unit, which)
        value = (image - ritz_val_ref[which] * coeff[which]) / (1.0 + kin[...])
        coeff[which] = value
        resid_ref[which] = value
        gath[which, my_band] = value
        spread(value, unit + 2)

        def go(step, carry):
            owner = lax.rem(my_band + step, n_band)
            pltpu.make_async_remote_copy(
                src_ref=gath.at[which, my_band],
                dst_ref=gath.at[which, my_band],
                send_sem=g_send.at[which],
                recv_sem=g_recv.at[which],
                device_id=(owner, my_grid),
                device_id_type=MESH,
            ).start()
            return carry

        lax.fori_loop(1, n_band, go, 0)

    def products(which):
        wait_bytes(gath.at[which, pl.ds(0, n_band - 1)], g_recv.at[which])

        def of_owner(owner, carry):
            there = gath[which, owner]
            for i in range(n_sub):
                both = basis_ref[i] * there
                acc[which, owner, i] = jnp.sum(both.reshape(N // 8, 8, N), axis=0)
            return carry

        lax.fori_loop(0, n_band, of_owner, 0)

    def send_products():
        count = 2 * n_band * n_sub
        summed = jnp.sum(acc[...].reshape(count, 8, N), axis=1)
        ones = jnp.ones((N, N), F32)
        spread_sum = jnp.dot(
            summed, ones, precision=lax.Precision.HIGHEST, preferred_element_type=F32
        )
        row = lax.broadcasted_iota(jnp.int32, (count, N), 0)
        column = lax.broadcasted_iota(jnp.int32, (count, N), 1)
        owner = lax.rem(row // n_sub, n_band)
        which = row // (n_sub * n_band)
        spread_sum = jnp.where(column == 2 * owner + which, spread_sum, 0.0)
        total_sum = spread_sum[0:n_sub]
        for k in range(1, 2 * n_band):
            total_sum = total_sum + spread_sum[k * n_sub:(k + 1) * n_sub]
        psend[...] = total_sum
        precv[my_grid] = total_sum

        def go(step, carry):
            peer = lax.rem(my_grid + step, n_grid)
            pltpu.make_async_remote_copy(
                src_ref=psend,
                dst_ref=precv.at[my_grid],
                send_sem=p_send,
                recv_sem=p_recv,
                device_id=(my_band, peer),
                device_id_type=MESH,
            ).start()
            return carry

        lax.fori_loop(1, n_grid, go, 0)

    ritz_ready(0)
    plane_inverse(0)
    ritz_ready(1)
    plane_forward(0)

    plane_inverse(1)
    residual(0)
    plane_forward(1)

    plane_inverse(2)
    residual(1)
    plane_forward(2)

    plane_inverse(3)
    hres_ref[0] = finish(2, 0)
    products(0)
    products(1)
    send_products()
    plane_forward(3)
    wait_bytes(precv.at[pl.ds(0, n_grid - 1)], p_recv)
    value = precv[0]
    for d in range(1, n_grid):
        value = value + precv[d]
    inter_ref[...] = value[:, 0:2 * n_band] / float(2 * N * total)
    hres_ref[1] = finish(3, 1)

    for which in range(2):
        wait_bytes(part.at[which, pl.ds(0, n_band - 1)], rs_send.at[which])
        wait_bytes(gath.at[which, pl.ds(0, n_band - 1)], g_send.at[which])
    for unit in range(4):
        wait_bytes(send_f.at[unit, pl.ds(0, N - slabs)], f_send.at[unit])
        wait_bytes(send_b.at[unit, pl.ds(0, N - slabs)], b_send.at[unit])
    wait_bytes(precv.at[pl.ds(0, n_grid - 1)], p_send)


def per_device(n_band, n_grid, basis, rotation, ritz_values, potential, col_map):
    n_sub = basis.shape[0]
    total = col_map.shape[0]
    slabs = N // n_grid
    inverse_z, forward_z, tables = make_tables()
    in_vmem = pl.BlockSpec(memory_space=pltpu.VMEM)
    in_smem = pl.BlockSpec(memory_space=pltpu.SMEM)
    own = (2, N, N)
    wide = (2 * slabs * LOW, total)
    rows = (slabs * N, 2 * N)
    cols = (2 * N, slabs * N)
    read = (2 * slabs * LOW, TOP * N)
    dma = pltpu.SemaphoreType.DMA
    resid, h_resid, inter = pl.pallas_call(
        functools.partial(kernel, n_band, n_grid, total),
        out_shape=(
            jax.ShapeDtypeStruct(own, F32),
            jax.ShapeDtypeStruct(own, F32),
            jax.ShapeDtypeStruct((n_sub, 2 * n_band), F32),
        ),
        in_specs=[in_vmem, in_smem, in_smem, in_vmem, in_vmem, in_vmem, in_vmem, in_vmem],
        out_specs=(in_vmem, in_vmem, in_vmem),
        scratch_shapes=[
            pltpu.VMEM((2, n_band, N, N), F32),
            pltpu.VMEM((2, n_band, N, N), F32),
            pltpu.VMEM((2, N, N), F32),
            pltpu.VMEM((N, N), F32),
            pltpu.VMEM((total, TOP * N), BF16),
            pltpu.VMEM((TOP * N, total), BF16),
            pltpu.VMEM((LOW, total), F32),
            pltpu.VMEM((N, N), F32),
            pltpu.VMEM((4, N, N), F32),
            pltpu.VMEM((4, N, N), F32),
            pltpu.VMEM((4, N, N), F32),
            pltpu.VMEM((4, N, N), F32),
            pltpu.VMEM((2 * slabs, total), F32),
            pltpu.VMEM(wide, BF16),
            pltpu.VMEM(wide, BF16),
            pltpu.VMEM(rows, BF16),
            pltpu.VMEM(rows, BF16),
            pltpu.VMEM(cols, BF16),
            pltpu.VMEM(cols, BF16),
            pltpu.VMEM(read, BF16),
            pltpu.VMEM(read, BF16),
            pltpu.VMEM((2, n_band, N, N), F32),
            pltpu.VMEM((2, n_band, n_sub, 8, N), F32),
            pltpu.VMEM((n_sub, N), F32),
            pltpu.VMEM((n_grid, n_sub, N), F32),
            dma((2,)), dma((2,)), dma((4,)), dma((4,)), dma((4,)), dma((4,)),
            dma((2,)), dma((2,)), dma, dma,
        ],
        compiler_params=pltpu.CompilerParams(
            collective_id=0, has_side_effects=True, vmem_limit_bytes=48 * 1024 * 1024
        ),
    )(
        basis.reshape(n_sub, N, N), rotation, ritz_values, potential,
        col_map.reshape(total // N, N), jnp.asarray(inverse_z), jnp.asarray(forward_z),
        jnp.asarray(tables),
    )
    shape = (2, 2, HALF, N)
    return resid.reshape(shape), h_resid.reshape(shape), inter


def solution(mesh):
    placed = (P("band", None, "grid", None), P(), P("band"), P("grid", None, None), P())
    return jax.shard_map(
        functools.partial(per_device, mesh.shape["band"], mesh.shape["grid"]),
        mesh=mesh,
        in_specs=placed,
        out_specs=(P("band", None, "grid", None), P("band", None, "grid", None), P("band", None)),
        check_vma=False,
    )
```

```python
import functools

import jax
import jax.numpy as jnp
import ml_dtypes
import numpy as np
from jax import lax
from jax.experimental import pallas as pl
from jax.experimental.pallas import tpu as pltpu
from jax.sharding import PartitionSpec as P

MESH = pl.DeviceIdType.MESH
N = 128
HALF = 64
LOW = 32
TOP = N // LOW
KINETIC_COEF = 2.0
PAIR = 2
SIDE = 4
F32 = jnp.float32
BF16 = jnp.bfloat16


def angle_tables():
    index = np.arange(N)
    angles = 2.0 * np.pi * (np.outer(index, index) % N) / N
    return np.cos(angles), np.sin(angles)


def split_table(table):
    high = table.astype(ml_dtypes.bfloat16)
    low = (table - high.astype(np.float64)).astype(ml_dtypes.bfloat16)
    return np.stack([high, low])


def make_tables():
    cosine, sine = angle_tables()
    inverse_z = (np.concatenate([cosine, sine], axis=1) / N).astype(np.float32)
    forward_z = np.concatenate([cosine, sine], axis=0).astype(np.float32)
    inverse = np.block([[cosine, sine], [-sine, cosine]]) / N
    forward = np.block([[cosine, -sine], [sine, cosine]])
    tables = np.concatenate(
        [split_table(inverse), split_table(inverse.T), split_table(forward), split_table(forward.T)]
    )
    return inverse_z, forward_z, tables


RIGHT_INV, LEFT_INV, RIGHT_FWD, LEFT_FWD = 0, 2, 4, 6


def grid_far(offset):
    x = offset // 4
    return (x if x < 3 else 1) + 2 * (offset // 2 % 2)


def band_far(offset):
    y = offset % 4
    return (y if y < 3 else 1) + offset // 4


def flip(index, offset):
    bit = 1
    while bit <= offset:
        if offset & bit:
            index = index + bit - 2 * bit * (index // bit % 2)
        bit *= 2
    return index


def far_first(index, count, far):
    order = sorted(range(1, count), key=lambda offset: -far(offset))
    return [flip(index, offset) for offset in order]


def split(value):
    high = value.astype(BF16)
    return high, (value - high.astype(F32)).astype(BF16)


def dot(left, right):
    return jnp.dot(left, right, preferred_element_type=F32)


def wait_bytes(view, sem):
    pltpu.make_async_copy(view, view, sem).wait()


def kernel(
    n_band, n_grid, total,
    basis_in, rot_in, ritz_val_in, pot_in, map_in, tzi_in, tzf_in, tab_in,
    resid_ref, hres_ref, inter_ref,
    part, rs, coeff, kin, onehot, onehot_t, mask, tmp,
    send_f, recv_f, send_b, recv_b,
    vals, wide, rows, read,
    gath, acc, psend, precv,
    basis_ref, rot_ref, ritz_val_ref, pot_ref, map_ref, tzi_ref, tzf_ref, tab_ref, in_sems,
    rs_send, rs_recv, f_send, f_recv, b_send, b_recv, g_send, g_recv, p_send, p_recv,
):
    slabs = N // n_grid
    chunks = total // N
    n_sub = basis_ref.shape[0]
    my_band = lax.axis_index("band")
    my_grid = lax.axis_index("grid")

    loads = [
        pltpu.make_async_copy(source, target, in_sems.at[k])
        for k, (source, target) in enumerate(
            (
                (rot_in, rot_ref),
                (basis_in, basis_ref),
                (map_in, map_ref),
                (tzi_in, tzi_ref),
                (tab_in, tab_ref),
                (pot_in, pot_ref),
                (tzf_in, tzf_ref),
                (ritz_val_in, ritz_val_ref),
            )
        )
    ]
    for load in loads:
        load.start()

    barrier = pltpu.get_barrier_semaphore()

    def greet_band(step, carry):
        peer = lax.rem(my_band + step, n_band)
        pl.semaphore_signal(barrier, inc=1, device_id=(peer, my_grid), device_id_type=MESH)
        return carry

    def greet_grid(step, carry):
        peer = lax.rem(my_grid + step, n_grid)
        pl.semaphore_signal(barrier, inc=1, device_id=(my_band, peer), device_id_type=MESH)
        return carry

    lax.fori_loop(1, n_band, greet_band, 0)
    lax.fori_loop(1, n_grid, greet_grid, 0)

    def partial_of(owner, which):
        column = owner * 2 + which
        row = my_band * n_sub
        value = rot_ref[column, row] * basis_ref[0]
        for i in range(1, n_sub):
            value = value + rot_ref[column, row + i] * basis_ref[i]
        return value

    loads[0].wait()
    loads[1].wait()
    started = False
    for which in range(2):
        for owner in far_first(my_band, n_band, band_far):
            part[which, owner] = partial_of(owner, which)
            if not started:
                pl.semaphore_wait(barrier, n_band - 1 + n_grid - 1)
                started = True
            pltpu.make_async_remote_copy(
                src_ref=part.at[which, owner],
                dst_ref=rs.at[which, my_band],
                send_sem=rs_send.at[which],
                recv_sem=rs_recv.at[which],
                device_id=(owner, my_grid),
                device_id_type=MESH,
            ).start()
        rs[which, my_band] = partial_of(my_band, which)
    loads[2].wait()

    lane_c = lax.broadcasted_iota(jnp.int32, (TOP * N, N), 0)
    lane_r = lax.broadcasted_iota(jnp.int32, (LOW, N), 0)
    for j in range(chunks):
        span = slice(j * N, (j + 1) * N)
        pos = map_ref[j:j + 1, :]
        x = lax.shift_right_logical(pos, 7)
        y = lax.bitwise_and(pos, N - 1)
        high = lax.shift_right_logical(x, 5) * N + y
        hit = jnp.where(lane_c == jnp.broadcast_to(high, lane_c.shape), 1.0, 0.0)
        onehot_t[:, span] = hit.astype(BF16)
        for t in range(TOP):
            onehot[span, t * N:(t + 1) * N] = hit[t * N:(t + 1) * N].T.astype(BF16)
        low = jnp.broadcast_to(lax.bitwise_and(x, LOW - 1), lane_r.shape)
        mask[:, span] = jnp.where(lane_r == low, 1.0, 0.0)

    mine = map_ref[pl.ds(my_grid // 2, 1), :].astype(F32)
    tmp[...] = jnp.broadcast_to(mine, (N, N)).T
    here = tmp[pl.ds(pl.multiple_of(lax.rem(my_grid, 2) * HALF, HALF), HALF), :].astype(jnp.int32)
    fx = lax.shift_right_logical(here, 7)
    fy = lax.bitwise_and(here, N - 1)
    fz = lax.broadcasted_iota(jnp.int32, (HALF, N), 1)
    fx = jnp.where(fx >= HALF, fx - N, fx)
    fy = jnp.where(fy >= HALF, fy - N, fy)
    fz = jnp.where(fz >= HALF, fz - N, fz)
    squares = (fx * fx + fy * fy + fz * fz).astype(F32)
    kinetic = squares * (KINETIC_COEF / float((N // 2) ** 2))
    kin[0:HALF] = kinetic
    kin[HALF:N] = kinetic

    for load in loads[3:]:
        load.wait()

    lane = lax.broadcasted_iota(jnp.int32, (slabs, N), 1)
    first = lane < HALF

    def exchange(send, recv, send_sem, recv_sem, unit):
        here_at = pl.multiple_of(my_grid * slabs, slabs)
        for peer in far_first(my_grid, n_grid, grid_far):
            there = pl.multiple_of(peer * slabs, slabs)
            pltpu.make_async_remote_copy(
                src_ref=send.at[unit, pl.ds(there, slabs)],
                dst_ref=recv.at[unit, pl.ds(here_at, slabs)],
                send_sem=send_sem.at[unit],
                recv_sem=recv_sem.at[unit],
                device_id=(my_band, peer),
                device_id_type=MESH,
            ).start()
        own = here_at
        recv[unit, pl.ds(own, slabs)] = send[unit, pl.ds(own, slabs)]

    def wait_exchange(recv, sem, unit):
        wait_bytes(recv.at[unit, pl.ds(0, N - slabs)], sem.at[unit])

    def spread(value, unit):
        real, imag = value[0:HALF], value[HALF:N]
        right = jnp.concatenate(
            [jnp.concatenate([real, -imag], axis=1), jnp.concatenate([imag, real], axis=1)], axis=0
        )
        send_f[unit] = lax.dot_general(
            tzi_ref[...], right, (((1,), (1,)), ((), ())),
            precision=lax.Precision.HIGHEST, preferred_element_type=F32,
        )
        exchange(send_f, recv_f, f_send, f_recv, unit)

    def ritz_ready(which):
        wait_bytes(rs.at[which, pl.ds(0, n_band - 1)], rs_recv.at[which])
        value = rs[which, 0]
        for d in range(1, n_band):
            value = value + rs[which, d]
        coeff[which] = value
        spread(value, which)

    def place_values(unit):
        wait_exchange(recv_f, f_recv, unit)
        for j in range(chunks):
            span = slice(j * N, (j + 1) * N)
            left = recv_f[unit, 2 * j * slabs:(2 * j + 1) * slabs]
            right = recv_f[unit, (2 * j + 1) * slabs:(2 * j + 2) * slabs]
            vals[0:slabs, span] = jnp.where(first, left, pltpu.roll(right, HALF, 1))
            vals[slabs:2 * slabs, span] = jnp.where(first, pltpu.roll(left, HALF, 1), right)
        chosen = mask[...] > 0.5
        for k in range(2 * slabs):
            row = vals[k:k + 1, :]
            high = row.astype(BF16).astype(F32)
            low = row - high
            span = slice(k * LOW, (k + 1) * LOW)
            wide[span] = jnp.where(chosen, jnp.broadcast_to(high, chosen.shape), 0.0).astype(BF16)
            span = slice((2 * slabs + k) * LOW, (2 * slabs + k + 1) * LOW)
            wide[span] = jnp.where(chosen, jnp.broadcast_to(low, chosen.shape), 0.0).astype(BF16)

    def place_columns():
        placed = dot(wide[...], onehot[...]).astype(BF16)
        for part_at in range(2):
            for q in range(2):
                for s in range(slabs):
                    k = (part_at * 2 + q) * slabs + s
                    for t in range(TOP):
                        rows[
                            s * N + t * LOW:s * N + (t + 1) * LOW,
                            (part_at * 2 + q) * N:(part_at * 2 + q + 1) * N,
                        ] = placed[k * LOW:(k + 1) * LOW, t * N:(t + 1) * N]

    def right_table(which, high, low):
        return dot(
            jnp.concatenate([high, low, high], axis=1),
            jnp.concatenate([tab_ref[which], tab_ref[which], tab_ref[which + 1]], axis=0),
        )

    def left_table(which, high, low):
        return dot(
            jnp.concatenate([tab_ref[which], tab_ref[which], tab_ref[which + 1]], axis=1),
            jnp.concatenate([high, low, high], axis=0),
        )

    def turn(value, to_columns):
        count = value.shape[0 if to_columns else 1] // N
        if to_columns:
            pieces = [[value[s * N:(s + 1) * N, q * N:(q + 1) * N] for s in range(count)] for q in range(2)]
        else:
            pieces = [[value[q * N:(q + 1) * N, s * N:(s + 1) * N] for q in range(2)] for s in range(count)]
        return jnp.concatenate([jnp.concatenate(line, axis=1) for line in pieces], axis=0)

    def transform():
        def some(g, carry):
            states = []
            for h in range(SIDE):
                at = (g * SIDE + h) * PAIR
                piece = pl.ds(pl.multiple_of(at * N, N), PAIR * N)
                states.append([rows[piece, 0:2 * N], rows[piece, 2 * N:4 * N]])
            for h in range(SIDE):
                states[h] = split(turn(right_table(RIGHT_INV, *states[h]), True))
            for h in range(SIDE):
                at = (g * SIDE + h) * PAIR
                field = left_table(LEFT_INV, *states[h])
                weights = jnp.concatenate([pot_ref[at + s] for s in range(PAIR)], axis=1)
                states[h] = split(field * jnp.concatenate([weights, weights], axis=0))
            for h in range(SIDE):
                states[h] = split(turn(left_table(LEFT_FWD, *states[h]), False))
            for h in range(SIDE):
                at = (g * SIDE + h) * PAIR
                both = split(right_table(RIGHT_FWD, *states[h]))
                for p in range(2):
                    for q in range(2):
                        for s in range(PAIR):
                            for t in range(TOP):
                                read[
                                    pl.ds(pl.multiple_of((q * slabs + at + s) * LOW, LOW), LOW),
                                    (p * TOP + t) * N:(p * TOP + t + 1) * N,
                                ] = both[p][s * N + t * LOW:s * N + (t + 1) * LOW, q * N:(q + 1) * N]
            return carry

        lax.fori_loop(0, slabs // (SIDE * PAIR), some, 0)

    def read_columns(unit):
        picked = dot(read[...], jnp.concatenate([onehot_t[...], onehot_t[...]], axis=0))
        for k in range(2 * slabs):
            vals[k:k + 1, :] = jnp.sum(
                picked[k * LOW:(k + 1) * LOW] * mask[...], axis=0, keepdims=True
            )
        for j in range(chunks):
            span = slice(j * N, (j + 1) * N)
            real = vals[0:slabs, span]
            imag = vals[slabs:2 * slabs, span]
            send_b[unit, 2 * j * slabs:(2 * j + 1) * slabs] = jnp.where(
                first, real, pltpu.roll(imag, HALF, 1)
            )
            send_b[unit, (2 * j + 1) * slabs:(2 * j + 2) * slabs] = jnp.where(
                first, pltpu.roll(real, HALF, 1), imag
            )

    def plane(unit):
        place_values(unit)
        place_columns()
        transform()
        read_columns(unit)
        exchange(send_b, recv_b, b_send, b_recv, unit)

    def finish(unit, which):
        wait_exchange(recv_b, b_recv, unit)
        turned = recv_b[unit].T
        real, imag = turned[0:HALF], turned[HALF:N]
        left = jnp.concatenate(
            [jnp.concatenate([real, imag], axis=1), jnp.concatenate([imag, -real], axis=1)], axis=0
        )
        value = jnp.dot(
            left, tzf_ref[...], precision=lax.Precision.HIGHEST, preferred_element_type=F32
        )
        return value + kin[...] * coeff[which]

    def residual(unit):
        which = unit
        image = finish(unit, which)
        value = (image - ritz_val_ref[which] * coeff[which]) / (1.0 + kin[...])
        coeff[which] = value
        resid_ref[which] = value
        gath[which, my_band] = value
        spread(value, unit + 2)


    def gather_copy(which, block, owner, sems):
        return pltpu.make_async_remote_copy(
            src_ref=gath.at[which, block],
            dst_ref=gath.at[which, block],
            send_sem=g_send.at[which, sems],
            recv_sem=g_recv.at[which, sems],
            device_id=(owner, my_grid),
            device_id_type=MESH,
        )

    ring = n_band // 2
    across = flip(my_band, ring)

    def gather_own(which):
        gather_copy(which, my_band, across, 0).start()
        for offset in range(ring - 1, 0, -1):
            gather_copy(which, my_band, flip(my_band, offset), 1).start()

    def gather_across(which):
        wait_bytes(gath.at[which, 0], g_recv.at[which, 0])
        for offset in range(ring - 1, 0, -1):
            gather_copy(which, across, flip(my_band, offset), 2).start()

    def products(which):
        for sems in (1, 2):
            wait_bytes(gath.at[which, pl.ds(0, ring - 1)], g_recv.at[which, sems])

        def of_owner(owner, carry):
            there = gath[which, owner]
            for i in range(n_sub):
                both = basis_ref[i] * there
                acc[which, owner, i] = jnp.sum(both.reshape(N // 8, 8, N), axis=0)
            return carry

        lax.fori_loop(0, n_band, of_owner, 0)

    def send_products():
        count = 2 * n_band * n_sub
        summed = jnp.sum(acc[...].reshape(count, 8, N), axis=1)
        ones = jnp.ones((N, N), F32)
        spread_sum = jnp.dot(
            summed, ones, precision=lax.Precision.HIGHEST, preferred_element_type=F32
        )
        row = lax.broadcasted_iota(jnp.int32, (count, N), 0)
        column = lax.broadcasted_iota(jnp.int32, (count, N), 1)
        owner = lax.rem(row // n_sub, n_band)
        which = row // (n_sub * n_band)
        spread_sum = jnp.where(column == 2 * owner + which, spread_sum, 0.0)
        total_sum = spread_sum[0:n_sub]
        for k in range(1, 2 * n_band):
            total_sum = total_sum + spread_sum[k * n_sub:(k + 1) * n_sub]
        psend[...] = total_sum
        precv[my_grid] = total_sum

        for peer in far_first(my_grid, n_grid, grid_far):
            pltpu.make_async_remote_copy(
                src_ref=psend,
                dst_ref=precv.at[my_grid],
                send_sem=p_send,
                recv_sem=p_recv,
                device_id=(my_band, peer),
                device_id_type=MESH,
            ).start()

    ritz_ready(0)
    ritz_ready(1)
    plane(0)
    plane(1)
    residual(0)
    gather_own(0)
    residual(1)
    gather_own(1)
    gather_across(0)
    plane(2)
    gather_across(1)
    plane(3)
    hres_ref[0] = finish(2, 0)
    products(0)
    products(1)
    send_products()
    hres_ref[1] = finish(3, 1)
    wait_bytes(precv.at[pl.ds(0, n_grid - 1)], p_recv)
    value = precv[0]
    for d in range(1, n_grid):
        value = value + precv[d]
    inter_ref[...] = value[:, 0:2 * n_band] / float(2 * N * total)

    for which in range(2):
        wait_bytes(part.at[which, pl.ds(0, n_band - 1)], rs_send.at[which])
        wait_bytes(gath.at[which, 0], g_send.at[which, 0])
        for sems in (1, 2):
            wait_bytes(gath.at[which, pl.ds(0, ring - 1)], g_send.at[which, sems])
    for unit in range(4):
        wait_bytes(send_f.at[unit, pl.ds(0, N - slabs)], f_send.at[unit])
        wait_bytes(send_b.at[unit, pl.ds(0, N - slabs)], b_send.at[unit])
    wait_bytes(precv.at[pl.ds(0, n_grid - 1)], p_send)


def per_device(n_band, n_grid, basis, rotation, ritz_values, potential, col_map):
    n_sub = basis.shape[0]
    total = col_map.shape[0]
    slabs = N // n_grid
    inverse_z, forward_z, tables = make_tables()
    in_vmem = pl.BlockSpec(memory_space=pltpu.VMEM)
    in_hbm = pl.BlockSpec(memory_space=pltpu.HBM)
    own = (2, N, N)
    wide = (4 * slabs * LOW, total)
    rows = (slabs * N, 4 * N)
    read = (2 * slabs * LOW, 2 * TOP * N)
    dma = pltpu.SemaphoreType.DMA
    resid, h_resid, inter = pl.pallas_call(
        functools.partial(kernel, n_band, n_grid, total),
        out_shape=(
            jax.ShapeDtypeStruct(own, F32),
            jax.ShapeDtypeStruct(own, F32),
            jax.ShapeDtypeStruct((n_sub, 2 * n_band), F32),
        ),
        in_specs=[in_hbm] * 8,
        out_specs=(in_vmem, in_vmem, in_vmem),
        scratch_shapes=[
            pltpu.VMEM((2, n_band, N, N), F32),
            pltpu.VMEM((2, n_band, N, N), F32),
            pltpu.VMEM((2, N, N), F32),
            pltpu.VMEM((N, N), F32),
            pltpu.VMEM((total, TOP * N), BF16),
            pltpu.VMEM((TOP * N, total), BF16),
            pltpu.VMEM((LOW, total), F32),
            pltpu.VMEM((N, N), F32),
            pltpu.VMEM((4, N, N), F32),
            pltpu.VMEM((4, N, N), F32),
            pltpu.VMEM((4, N, N), F32),
            pltpu.VMEM((4, N, N), F32),
            pltpu.VMEM((2 * slabs, total), F32),
            pltpu.VMEM(wide, BF16),
            pltpu.VMEM(rows, BF16),
            pltpu.VMEM(read, BF16),
            pltpu.VMEM((2, n_band, N, N), F32),
            pltpu.VMEM((2, n_band, n_sub, 8, N), F32),
            pltpu.VMEM((n_sub, N), F32),
            pltpu.VMEM((n_grid, n_sub, N), F32),
            pltpu.VMEM((n_sub, N, N), F32),
            pltpu.SMEM((2 * n_band, n_band * n_sub), F32),
            pltpu.SMEM((2,), F32),
            pltpu.VMEM((slabs, N, N), F32),
            pltpu.VMEM((total // N, N), jnp.int32),
            pltpu.VMEM((N, 2 * N), F32),
            pltpu.VMEM((2 * N, N), F32),
            pltpu.VMEM((8, 2 * N, 2 * N), BF16),
            dma((8,)),
            dma((2,)), dma((2,)), dma((4,)), dma((4,)), dma((4,)), dma((4,)),
            dma((2, 3)), dma((2, 3)), dma, dma,
        ],
        compiler_params=pltpu.CompilerParams(
            collective_id=0, has_side_effects=True, vmem_limit_bytes=56 * 1024 * 1024
        ),
    )(
        basis.reshape(n_sub, N, N), rotation.T, ritz_values, potential,
        col_map.reshape(total // N, N), jnp.asarray(inverse_z), jnp.asarray(forward_z),
        jnp.asarray(tables),
    )
    shape = (2, 2, HALF, N)
    return resid.reshape(shape), h_resid.reshape(shape), inter


def solution(mesh):
    placed = (P("band", None, "grid", None), P(), P("band"), P("grid", None, None), P())
    return jax.shard_map(
        functools.partial(per_device, mesh.shape["band"], mesh.shape["grid"]),
        mesh=mesh,
        in_specs=placed,
        out_specs=(P("band", None, "grid", None), P("band", None, "grid", None), P("band", None)),
        check_vma=False,
    )
```

```python
import functools

import jax
import jax.numpy as jnp
import ml_dtypes
import numpy as np
from jax import lax
from jax.experimental import pallas as pl
from jax.experimental.pallas import tpu as pltpu
from jax.sharding import PartitionSpec as P

MESH = pl.DeviceIdType.MESH
N = 128
HALF = 64
LOW = 32
TOP = N // LOW
KINETIC_COEF = 2.0
PAIR = 2
SIDE = 4
F32 = jnp.float32
BF16 = jnp.bfloat16


def angle_tables():
    index = np.arange(N)
    angles = 2.0 * np.pi * (np.outer(index, index) % N) / N
    return np.cos(angles), np.sin(angles)


def split_table(table):
    high = table.astype(ml_dtypes.bfloat16)
    low = (table - high.astype(np.float64)).astype(ml_dtypes.bfloat16)
    return np.stack([high, low])


def make_tables():
    cosine, sine = angle_tables()
    high, low = split_table(np.concatenate([cosine, sine], axis=1) / N)
    inverse_z = np.concatenate([high, low, high], axis=1)
    high, low = split_table(np.concatenate([cosine, sine], axis=0))
    forward_z = np.concatenate([high, low, high], axis=0)
    inverse = np.block([[cosine, sine], [-sine, cosine]]) / N
    forward = np.block([[cosine, -sine], [sine, cosine]])
    tables = np.concatenate(
        [split_table(inverse), split_table(inverse.T), split_table(forward), split_table(forward.T)]
    )
    return inverse_z, forward_z, tables


RIGHT_INV, LEFT_INV, RIGHT_FWD, LEFT_FWD = 0, 2, 4, 6


def grid_far(offset):
    x = offset // 4
    return (x if x < 3 else 1) + 2 * (offset // 2 % 2)


def band_far(offset):
    y = offset % 4
    return (y if y < 3 else 1) + offset // 4


def flip(index, offset):
    bit = 1
    while bit <= offset:
        if offset & bit:
            index = index + bit - 2 * bit * (index // bit % 2)
        bit *= 2
    return index


def far_first(index, count, far):
    order = sorted(range(1, count), key=lambda offset: -far(offset))
    return [flip(index, offset) for offset in order]


def split(value):
    high = value.astype(BF16)
    return high, (value - high.astype(F32)).astype(BF16)


def dot(left, right):
    return jnp.dot(left, right, preferred_element_type=F32)


def wait_bytes(view, sem):
    pltpu.make_async_copy(view, view, sem).wait()


def kernel(
    n_band, n_grid, total,
    basis_in, rot_in, ritz_val_in, pot_in, map_in, tzi_in, tzf_in, tab_in,
    resid_out, hres_out, inter_out,
    hres_ref, inter_ref, out_sems,
    part, rs, coeff, kin, onehot, onehot_t, mask, tmp,
    send_f, recv_f, send_b, recv_b,
    vals, wide, rows, read,
    gath, acc, psend, precv,
    basis_ref, rot_ref, ritz_val_ref, pot_ref, map_ref, tzi_ref, tzf_ref, tab_ref, in_sems,
    rs_send, rs_recv, f_send, f_recv, b_send, b_recv, g_send, g_recv, p_send, p_recv,
):
    slabs = N // n_grid
    chunks = total // N
    n_sub = basis_ref.shape[0]
    my_band = lax.axis_index("band")
    my_grid = lax.axis_index("grid")

    loads = [
        pltpu.make_async_copy(source, target, in_sems.at[k])
        for k, (source, target) in enumerate(
            (
                (rot_in, rot_ref),
                (basis_in, basis_ref),
                (map_in, map_ref),
                (tzi_in, tzi_ref),
                (tab_in, tab_ref),
                (pot_in, pot_ref),
                (tzf_in, tzf_ref),
                (ritz_val_in, ritz_val_ref),
            )
        )
    ]
    barrier = pltpu.get_barrier_semaphore()

    def greet_band(step, carry):
        peer = lax.rem(my_band + step, n_band)
        pl.semaphore_signal(barrier, inc=1, device_id=(peer, my_grid), device_id_type=MESH)
        return carry

    def greet_grid(step, carry):
        peer = lax.rem(my_grid + step, n_grid)
        pl.semaphore_signal(barrier, inc=1, device_id=(my_band, peer), device_id_type=MESH)
        return carry

    lax.fori_loop(1, n_band, greet_band, 0)
    lax.fori_loop(1, n_grid, greet_grid, 0)
    for load in loads:
        load.start()

    def partial_of(owner, which):
        column = owner * 2 + which
        row = my_band * n_sub
        value = rot_ref[column, row] * basis_ref[0]
        for i in range(1, n_sub):
            value = value + rot_ref[column, row + i] * basis_ref[i]
        return value

    loads[0].wait()
    loads[1].wait()
    started = False
    for which in range(2):
        for owner in far_first(my_band, n_band, band_far):
            part[which, owner] = partial_of(owner, which)
            if not started:
                pl.semaphore_wait(barrier, n_band - 1 + n_grid - 1)
                started = True
            pltpu.make_async_remote_copy(
                src_ref=part.at[which, owner],
                dst_ref=rs.at[which, my_band],
                send_sem=rs_send.at[which],
                recv_sem=rs_recv.at[which],
                device_id=(owner, my_grid),
                device_id_type=MESH,
            ).start()
        rs[which, my_band] = partial_of(my_band, which)
    loads[2].wait()

    lane_c = lax.broadcasted_iota(jnp.int32, (TOP * N, N), 0)
    lane_r = lax.broadcasted_iota(jnp.int32, (LOW, N), 0)
    for j in range(chunks):
        span = slice(j * N, (j + 1) * N)
        pos = map_ref[j:j + 1, :]
        x = lax.shift_right_logical(pos, 7)
        y = lax.bitwise_and(pos, N - 1)
        high = lax.shift_right_logical(x, 5) * N + y
        hit = jnp.where(lane_c == jnp.broadcast_to(high, lane_c.shape), 1.0, 0.0)
        onehot_t[:, span] = hit.astype(BF16)
        for t in range(TOP):
            onehot[span, t * N:(t + 1) * N] = hit[t * N:(t + 1) * N].T.astype(BF16)
        low = jnp.broadcast_to(lax.bitwise_and(x, LOW - 1), lane_r.shape)
        mask[:, span] = jnp.where(lane_r == low, 1.0, 0.0)

    mine = map_ref[pl.ds(my_grid // 2, 1), :].astype(F32)
    tmp[...] = jnp.broadcast_to(mine, (N, N)).T
    here = tmp[pl.ds(pl.multiple_of(lax.rem(my_grid, 2) * HALF, HALF), HALF), :].astype(jnp.int32)
    fx = lax.shift_right_logical(here, 7)
    fy = lax.bitwise_and(here, N - 1)
    fz = lax.broadcasted_iota(jnp.int32, (HALF, N), 1)
    fx = jnp.where(fx >= HALF, fx - N, fx)
    fy = jnp.where(fy >= HALF, fy - N, fy)
    fz = jnp.where(fz >= HALF, fz - N, fz)
    squares = (fx * fx + fy * fy + fz * fz).astype(F32)
    kinetic = squares * (KINETIC_COEF / float((N // 2) ** 2))
    kin[0:HALF] = kinetic
    kin[HALF:N] = kinetic

    for load in loads[3:]:
        load.wait()

    lane = lax.broadcasted_iota(jnp.int32, (slabs, N), 1)
    first = lane < HALF

    def exchange(send, recv, send_sem, recv_sem, unit):
        here_at = pl.multiple_of(my_grid * slabs, slabs)
        for peer in far_first(my_grid, n_grid, grid_far):
            there = pl.multiple_of(peer * slabs, slabs)
            pltpu.make_async_remote_copy(
                src_ref=send.at[unit, pl.ds(there, slabs)],
                dst_ref=recv.at[unit, pl.ds(here_at, slabs)],
                send_sem=send_sem.at[unit],
                recv_sem=recv_sem.at[unit],
                device_id=(my_band, peer),
                device_id_type=MESH,
            ).start()
        own = here_at
        recv[unit, pl.ds(own, slabs)] = send[unit, pl.ds(own, slabs)]

    def wait_exchange(recv, sem, unit):
        wait_bytes(recv.at[unit, pl.ds(0, N - slabs)], sem.at[unit])

    def spread(value, unit):
        real, imag = value[0:HALF], value[HALF:N]
        right = jnp.concatenate(
            [jnp.concatenate([real, -imag], axis=1), jnp.concatenate([imag, real], axis=1)], axis=0
        )
        high, low = split(right)
        send_f[unit] = lax.dot_general(
            tzi_ref[...], jnp.concatenate([high, high, low], axis=1), (((1,), (1,)), ((), ())),
            preferred_element_type=F32,
        )
        exchange(send_f, recv_f, f_send, f_recv, unit)

    def ritz_ready(which):
        wait_bytes(rs.at[which, pl.ds(0, n_band - 1)], rs_recv.at[which])
        value = rs[which, 0]
        for d in range(1, n_band):
            value = value + rs[which, d]
        coeff[which] = value
        spread(value, which)

    def place_values(unit):
        wait_exchange(recv_f, f_recv, unit)
        for j in range(chunks):
            span = slice(j * N, (j + 1) * N)
            left = recv_f[unit, 2 * j * slabs:(2 * j + 1) * slabs]
            right = recv_f[unit, (2 * j + 1) * slabs:(2 * j + 2) * slabs]
            vals[0:slabs, span] = jnp.where(first, left, pltpu.roll(right, HALF, 1))
            vals[slabs:2 * slabs, span] = jnp.where(first, pltpu.roll(left, HALF, 1), right)
        chosen = mask[...] > 0.5
        for k in range(2 * slabs):
            row = vals[k:k + 1, :]
            high = row.astype(BF16).astype(F32)
            low = row - high
            span = slice(k * LOW, (k + 1) * LOW)
            wide[span] = jnp.where(chosen, jnp.broadcast_to(high, chosen.shape), 0.0).astype(BF16)
            span = slice((2 * slabs + k) * LOW, (2 * slabs + k + 1) * LOW)
            wide[span] = jnp.where(chosen, jnp.broadcast_to(low, chosen.shape), 0.0).astype(BF16)

    def place_columns():
        placed = dot(wide[...], onehot[...]).astype(BF16)
        for part_at in range(2):
            for q in range(2):
                for s in range(slabs):
                    k = (part_at * 2 + q) * slabs + s
                    for t in range(TOP):
                        rows[
                            s * N + t * LOW:s * N + (t + 1) * LOW,
                            (part_at * 2 + q) * N:(part_at * 2 + q + 1) * N,
                        ] = placed[k * LOW:(k + 1) * LOW, t * N:(t + 1) * N]

    def right_table(which, high, low):
        return dot(
            jnp.concatenate([high, low, high], axis=1),
            jnp.concatenate([tab_ref[which], tab_ref[which], tab_ref[which + 1]], axis=0),
        )

    def left_table(which, high, low):
        return dot(
            jnp.concatenate([tab_ref[which], tab_ref[which], tab_ref[which + 1]], axis=1),
            jnp.concatenate([high, low, high], axis=0),
        )

    def turn(value, to_columns):
        count = value.shape[0 if to_columns else 1] // N
        if to_columns:
            pieces = [[value[s * N:(s + 1) * N, q * N:(q + 1) * N] for s in range(count)] for q in range(2)]
        else:
            pieces = [[value[q * N:(q + 1) * N, s * N:(s + 1) * N] for q in range(2)] for s in range(count)]
        return jnp.concatenate([jnp.concatenate(line, axis=1) for line in pieces], axis=0)

    def transform():
        def some(g, carry):
            states = []
            for h in range(SIDE):
                at = (g * SIDE + h) * PAIR
                piece = pl.ds(pl.multiple_of(at * N, N), PAIR * N)
                states.append([rows[piece, 0:2 * N], rows[piece, 2 * N:4 * N]])
            for h in range(SIDE):
                states[h] = split(turn(right_table(RIGHT_INV, *states[h]), True))
            for h in range(SIDE):
                at = (g * SIDE + h) * PAIR
                field = left_table(LEFT_INV, *states[h])
                weights = jnp.concatenate([pot_ref[at + s] for s in range(PAIR)], axis=1)
                states[h] = split(field * jnp.concatenate([weights, weights], axis=0))
            for h in range(SIDE):
                states[h] = split(turn(left_table(LEFT_FWD, *states[h]), False))
            for h in range(SIDE):
                at = (g * SIDE + h) * PAIR
                both = split(right_table(RIGHT_FWD, *states[h]))
                for p in range(2):
                    for q in range(2):
                        for s in range(PAIR):
                            for t in range(TOP):
                                read[
                                    pl.ds(pl.multiple_of((q * slabs + at + s) * LOW, LOW), LOW),
                                    (p * TOP + t) * N:(p * TOP + t + 1) * N,
                                ] = both[p][s * N + t * LOW:s * N + (t + 1) * LOW, q * N:(q + 1) * N]
            return carry

        lax.fori_loop(0, slabs // (SIDE * PAIR), some, 0)

    def read_columns(unit):
        picked = dot(read[...], jnp.concatenate([onehot_t[...], onehot_t[...]], axis=0))
        for k in range(2 * slabs):
            vals[k:k + 1, :] = jnp.sum(
                picked[k * LOW:(k + 1) * LOW] * mask[...], axis=0, keepdims=True
            )
        for j in range(chunks):
            span = slice(j * N, (j + 1) * N)
            real = vals[0:slabs, span]
            imag = vals[slabs:2 * slabs, span]
            send_b[unit, 2 * j * slabs:(2 * j + 1) * slabs] = jnp.where(
                first, real, pltpu.roll(imag, HALF, 1)
            )
            send_b[unit, (2 * j + 1) * slabs:(2 * j + 2) * slabs] = jnp.where(
                first, pltpu.roll(real, HALF, 1), imag
            )

    def plane_start(unit):
        place_values(unit)
        place_columns()
        transform()

    def plane_end(unit):
        read_columns(unit)
        exchange(send_b, recv_b, b_send, b_recv, unit)

    def plane(unit):
        plane_start(unit)
        plane_end(unit)

    def finish(unit, which):
        wait_exchange(recv_b, b_recv, unit)
        turned = recv_b[unit].T
        real, imag = turned[0:HALF], turned[HALF:N]
        left = jnp.concatenate(
            [jnp.concatenate([real, imag], axis=1), jnp.concatenate([imag, -real], axis=1)], axis=0
        )
        high, low = split(left)
        value = dot(jnp.concatenate([high, high, low], axis=1), tzf_ref[...])
        return value + kin[...] * coeff[which]

    def residual(unit):
        which = unit
        image = finish(unit, which)
        value = (image - ritz_val_ref[which] * coeff[which]) / (1.0 + kin[...])
        coeff[which] = value
        spread(value, unit + 2)
        gath[which, my_band] = value
        pltpu.make_async_copy(gath.at[which, my_band], resid_out.at[which], out_sems.at[which]).start()


    def gather_copy(which, block, owner, sems):
        return pltpu.make_async_remote_copy(
            src_ref=gath.at[which, block],
            dst_ref=gath.at[which, block],
            send_sem=g_send.at[which, sems],
            recv_sem=g_recv.at[which, sems],
            device_id=(owner, my_grid),
            device_id_type=MESH,
        )

    ring = n_band // 2
    across = flip(my_band, ring)

    def gather_own(which):
        gather_copy(which, my_band, across, 0).start()
        for offset in range(ring - 1, 0, -1):
            gather_copy(which, my_band, flip(my_band, offset), 1).start()

    def gather_across(which):
        wait_bytes(gath.at[which, 0], g_recv.at[which, 0])
        for offset in range(ring - 1, 0, -1):
            gather_copy(which, across, flip(my_band, offset), 2).start()

    def products(which):
        for sems in (1, 2):
            wait_bytes(gath.at[which, pl.ds(0, ring - 1)], g_recv.at[which, sems])

        lines = []
        for owner in range(n_band):
            there = gath[which, owner]
            for i in range(n_sub):
                lines.append(jnp.sum(basis_ref[i] * there, axis=0, keepdims=True))
        high, low = split(jnp.concatenate(lines, axis=0))
        every = dot(jnp.concatenate([high, low], axis=1), jnp.ones((2 * N, N), BF16))
        lanes = lax.broadcasted_iota(jnp.int32, (n_sub, N), 1)
        found = jnp.zeros((n_sub, N), F32)
        for owner in range(n_band):
            found = jnp.where(lanes == 2 * owner + which, every[owner * n_sub:(owner + 1) * n_sub], found)
        acc[which] = found

    def send_products():
        total_sum = acc[0] + acc[1]
        psend[...] = total_sum
        precv[my_grid] = total_sum

        for peer in far_first(my_grid, n_grid, grid_far):
            pltpu.make_async_remote_copy(
                src_ref=psend,
                dst_ref=precv.at[my_grid],
                send_sem=p_send,
                recv_sem=p_recv,
                device_id=(my_band, peer),
                device_id_type=MESH,
            ).start()

    ritz_ready(0)
    ritz_ready(1)
    def first_planes(unit, carry):
        plane(unit)
        return carry

    lax.fori_loop(0, 2, first_planes, 0)
    residual(0)
    gather_own(0)
    gather_across(0)
    residual(1)
    gather_own(1)
    def last_planes(unit, carry):
        plane(unit)

        @pl.when(unit == 2)
        def _():
            gather_across(1)

        return carry

    lax.fori_loop(2, 4, last_planes, 0)
    products(0)
    products(1)
    send_products()
    hres_ref[0] = finish(2, 0)
    pltpu.make_async_copy(hres_ref.at[0], hres_out.at[0], out_sems.at[2]).start()
    hres_ref[1] = finish(3, 1)
    pltpu.make_async_copy(hres_ref.at[1], hres_out.at[1], out_sems.at[3]).start()
    wait_bytes(precv.at[pl.ds(0, n_grid - 1)], p_recv)
    value = precv[0]
    for d in range(1, n_grid):
        value = value + precv[d]
    inter_ref[...] = value / float(2 * N * total)
    pltpu.make_async_copy(inter_ref, inter_out, out_sems.at[4]).start()

    for which in range(2):
        wait_bytes(part.at[which, pl.ds(0, n_band - 1)], rs_send.at[which])
        wait_bytes(gath.at[which, 0], g_send.at[which, 0])
        for sems in (1, 2):
            wait_bytes(gath.at[which, pl.ds(0, ring - 1)], g_send.at[which, sems])
    for unit in range(4):
        wait_bytes(send_f.at[unit, pl.ds(0, N - slabs)], f_send.at[unit])
        wait_bytes(send_b.at[unit, pl.ds(0, N - slabs)], b_send.at[unit])
    wait_bytes(precv.at[pl.ds(0, n_grid - 1)], p_send)
    for which in range(2):
        pltpu.make_async_copy(gath.at[which, my_band], resid_out.at[which], out_sems.at[which]).wait()
        pltpu.make_async_copy(hres_ref.at[which], hres_out.at[which], out_sems.at[2 + which]).wait()
    pltpu.make_async_copy(inter_ref, inter_out, out_sems.at[4]).wait()


def hand_out(resid_in, hres_in, inter_in, resid_out, hres_out, inter_out, held, held_inter, sems):
    there = [
        pltpu.make_async_copy(inter_in, held_inter, sems.at[0, 0]),
        pltpu.make_async_copy(hres_in, held.at[0], sems.at[0, 1]),
        pltpu.make_async_copy(resid_in, held.at[1], sems.at[0, 2]),
    ]
    back = [
        pltpu.make_async_copy(held.at[0], hres_out, sems.at[1, 1]),
        pltpu.make_async_copy(held.at[1], resid_out, sems.at[1, 2]),
    ]
    for copy in there:
        copy.start()
    there[0].wait()
    inter_out[...] = held_inter[:, 0:inter_out.shape[1]]
    for k in range(2):
        there[1 + k].wait()
        back[k].start()
    for copy in back:
        copy.wait()


def per_device(n_band, n_grid, basis, rotation, ritz_values, potential, col_map):
    n_sub = basis.shape[0]
    total = col_map.shape[0]
    slabs = N // n_grid
    inverse_z, forward_z, tables = make_tables()
    in_vmem = pl.BlockSpec(memory_space=pltpu.VMEM)
    in_hbm = pl.BlockSpec(memory_space=pltpu.HBM)
    own = (2, N, N)
    wide = (4 * slabs * LOW, total)
    rows = (slabs * N, 4 * N)
    read = (2 * slabs * LOW, 2 * TOP * N)
    dma = pltpu.SemaphoreType.DMA
    resid, h_resid, inter = pl.pallas_call(
        functools.partial(kernel, n_band, n_grid, total),
        out_shape=(
            jax.ShapeDtypeStruct(own, F32),
            jax.ShapeDtypeStruct(own, F32),
            jax.ShapeDtypeStruct((n_sub, N), F32),
        ),
        in_specs=[in_hbm] * 8,
        out_specs=(in_hbm, in_hbm, in_hbm),
        scratch_shapes=[
            pltpu.VMEM((2, N, N), F32),
            pltpu.VMEM((n_sub, N), F32),
            dma((5,)),
            pltpu.VMEM((2, n_band, N, N), F32),
            pltpu.VMEM((2, n_band, N, N), F32),
            pltpu.VMEM((2, N, N), F32),
            pltpu.VMEM((N, N), F32),
            pltpu.VMEM((total, TOP * N), BF16),
            pltpu.VMEM((TOP * N, total), BF16),
            pltpu.VMEM((LOW, total), F32),
            pltpu.VMEM((N, N), F32),
            pltpu.VMEM((4, N, N), F32),
            pltpu.VMEM((4, N, N), F32),
            pltpu.VMEM((4, N, N), F32),
            pltpu.VMEM((4, N, N), F32),
            pltpu.VMEM((2 * slabs, total), F32),
            pltpu.VMEM(wide, BF16),
            pltpu.VMEM(rows, BF16),
            pltpu.VMEM(read, BF16),
            pltpu.VMEM((2, n_band, N, N), F32),
            pltpu.VMEM((2, n_sub, N), F32),
            pltpu.VMEM((n_sub, N), F32),
            pltpu.VMEM((n_grid, n_sub, N), F32),
            pltpu.VMEM((n_sub, N, N), F32),
            pltpu.SMEM((2 * n_band, n_band * n_sub), F32),
            pltpu.SMEM((2,), F32),
            pltpu.VMEM((slabs, N, N), F32),
            pltpu.VMEM((total // N, N), jnp.int32),
            pltpu.VMEM((N, 6 * N), BF16),
            pltpu.VMEM((6 * N, N), BF16),
            pltpu.VMEM((8, 2 * N, 2 * N), BF16),
            dma((8,)),
            dma((2,)), dma((2,)), dma((4,)), dma((4,)), dma((4,)), dma((4,)),
            dma((2, 3)), dma((2, 3)), dma, dma,
        ],
        compiler_params=pltpu.CompilerParams(
            collective_id=0, has_side_effects=True, vmem_limit_bytes=56 * 1024 * 1024
        ),
    )(
        basis.reshape(n_sub, N, N), rotation.T, ritz_values, potential,
        col_map.reshape(total // N, N), jnp.asarray(inverse_z), jnp.asarray(forward_z),
        jnp.asarray(tables),
    )
    resid, h_resid, inter = pl.pallas_call(
        hand_out,
        out_shape=(
            jax.ShapeDtypeStruct(own, F32),
            jax.ShapeDtypeStruct(own, F32),
            jax.ShapeDtypeStruct((n_sub, 2 * n_band), F32),
        ),
        in_specs=[in_hbm] * 3,
        out_specs=(in_hbm, in_hbm, in_vmem),
        scratch_shapes=[pltpu.VMEM((2,) + own, F32), pltpu.VMEM((n_sub, N), F32), dma((2, 3))],
        compiler_params=pltpu.CompilerParams(vmem_limit_bytes=56 * 1024 * 1024),
    )(resid, h_resid, inter)
    shape = (2, 2, HALF, N)
    return resid.reshape(shape), h_resid.reshape(shape), inter


def solution(mesh):
    placed = (P("band", None, "grid", None), P(), P("band"), P("grid", None, None), P())
    return jax.shard_map(
        functools.partial(per_device, mesh.shape["band"], mesh.shape["grid"]),
        mesh=mesh,
        in_specs=placed,
        out_specs=(P("band", None, "grid", None), P("band", None, "grid", None), P("band", None)),
        check_vma=False,
    )
```

```python
import functools

import jax
import jax.numpy as jnp
import ml_dtypes
import numpy as np
from jax import lax
from jax.experimental import pallas as pl
from jax.experimental.pallas import tpu as pltpu
from jax.sharding import PartitionSpec as P

MESH = pl.DeviceIdType.MESH
N = 128
HALF = 64
LOW = 32
TOP = N // LOW
KINETIC_COEF = 2.0
PAIR = 2
SIDE = 4
F32 = jnp.float32
BF16 = jnp.bfloat16


def angle_tables():
    index = np.arange(N)
    angles = 2.0 * np.pi * (np.outer(index, index) % N) / N
    return np.cos(angles), np.sin(angles)


def split_table(table):
    high = table.astype(ml_dtypes.bfloat16)
    low = (table - high.astype(np.float64)).astype(ml_dtypes.bfloat16)
    return np.stack([high, low])


def make_tables():
    cosine, sine = angle_tables()
    high, low = split_table(np.concatenate([cosine, sine], axis=1) / N)
    inverse_z = np.concatenate([high, low, high], axis=1)
    high, low = split_table(np.concatenate([cosine, sine], axis=0))
    forward_z = np.concatenate([high, low, high], axis=0)
    inverse = np.block([[cosine, sine], [-sine, cosine]]) / N
    forward = np.block([[cosine, -sine], [sine, cosine]])
    tables = np.concatenate(
        [split_table(inverse), split_table(inverse.T), split_table(forward), split_table(forward.T)]
    )
    return inverse_z, forward_z, tables


RIGHT_INV, LEFT_INV, RIGHT_FWD, LEFT_FWD = 0, 2, 4, 6


def grid_far(offset):
    x = offset // 4
    return (x if x < 3 else 1) + 2 * (offset // 2 % 2)


def band_far(offset):
    y = offset % 4
    return (y if y < 3 else 1) + offset // 4


def flip(index, offset):
    bit = 1
    while bit <= offset:
        if offset & bit:
            index = index + bit - 2 * bit * (index // bit % 2)
        bit *= 2
    return index


def far_first(index, count, far):
    order = sorted(range(1, count), key=lambda offset: -far(offset))
    return [flip(index, offset) for offset in order]


def split(value):
    high = value.astype(BF16)
    return high, (value - high.astype(F32)).astype(BF16)


def dot(left, right):
    return jnp.dot(left, right, preferred_element_type=F32)


def wait_bytes(view, sem):
    pltpu.make_async_copy(view, view, sem).wait()


def kernel(
    n_band, n_grid, total,
    basis_in, rot_in, ritz_val_in, pot_in, map_in, tzi_in, tzf_in, tab_in,
    resid_out, hres_out, inter_out,
    hres_ref, inter_ref, out_sems,
    part, rs, coeff, kin, onehot, onehot_t, mask, tmp,
    send_f, recv_f, send_b, recv_b,
    vals, wide, rows, read,
    gath, psend, precv,
    basis_ref, rot_ref, ritz_val_ref, pot_ref, map_ref, tzi_ref, tzf_ref, tab_ref, in_sems,
    rs_send, rs_recv, f_send, f_recv, b_send, b_recv, g_send, g_recv, p_send, p_recv,
):
    slabs = N // n_grid
    chunks = total // N
    n_sub = basis_ref.shape[0]
    my_band = lax.axis_index("band")
    my_grid = lax.axis_index("grid")

    loads = [
        pltpu.make_async_copy(source, target, in_sems.at[k])
        for k, (source, target) in enumerate(
            (
                (rot_in, rot_ref),
                (map_in, map_ref),
                (tzi_in, tzi_ref),
                (tab_in, tab_ref),
                (pot_in, pot_ref),
                (tzf_in, tzf_ref),
                (ritz_val_in, ritz_val_ref),
            )
        )
    ]
    barrier = pltpu.get_barrier_semaphore()

    for peer in far_first(my_grid, n_grid, grid_far):
        pl.semaphore_signal(barrier, inc=1, device_id=(my_band, peer), device_id_type=MESH)
    for peer in far_first(my_band, n_band, band_far):
        pl.semaphore_signal(barrier, inc=1, device_id=(peer, my_grid), device_id_type=MESH)
    quarter = n_sub // 4
    basis_loads = [
        pltpu.make_async_copy(
            basis_in.at[pl.ds(k * quarter, quarter)],
            basis_ref.at[pl.ds(k * quarter, quarter)],
            in_sems.at[len(loads) + k],
        )
        for k in range(4)
    ]
    for load in loads[:1] + basis_loads + loads[1:]:
        load.start()

    def partial_of(owner, which):
        column = owner * 2 + which
        row = my_band * n_sub
        value = rot_ref[column, row] * basis_ref[0]
        for i in range(1, n_sub):
            value = value + rot_ref[column, row + i] * basis_ref[i]
        return value

    for load in loads[:1] + basis_loads:
        load.wait()
    started = False
    for which in range(2):
        for owner in far_first(my_band, n_band, band_far):
            part[which, owner] = partial_of(owner, which)
            if not started:
                pl.semaphore_wait(barrier, n_band - 1 + n_grid - 1)
                started = True
            pltpu.make_async_remote_copy(
                src_ref=part.at[which, owner],
                dst_ref=rs.at[which, my_band],
                send_sem=rs_send.at[which],
                recv_sem=rs_recv.at[which],
                device_id=(owner, my_grid),
                device_id_type=MESH,
            ).start()
        rs[which, my_band] = partial_of(my_band, which)
    loads[1].wait()

    lane_c = lax.broadcasted_iota(jnp.int32, (TOP * N, N), 0)
    lane_r = lax.broadcasted_iota(jnp.int32, (LOW, N), 0)
    for j in range(chunks):
        span = slice(j * N, (j + 1) * N)
        pos = map_ref[j:j + 1, :]
        x = lax.shift_right_logical(pos, 7)
        y = lax.bitwise_and(pos, N - 1)
        high = lax.shift_right_logical(x, 5) * N + y
        hit = jnp.where(lane_c == jnp.broadcast_to(high, lane_c.shape), 1.0, 0.0)
        onehot_t[:, span] = hit.astype(BF16)
        for t in range(TOP):
            onehot[span, t * N:(t + 1) * N] = hit[t * N:(t + 1) * N].T.astype(BF16)
        low = jnp.broadcast_to(lax.bitwise_and(x, LOW - 1), lane_r.shape)
        mask[:, span] = jnp.where(lane_r == low, 1.0, 0.0)

    mine = map_ref[pl.ds(my_grid // 2, 1), :].astype(F32)
    tmp[...] = jnp.broadcast_to(mine, (N, N)).T
    here = tmp[pl.ds(pl.multiple_of(lax.rem(my_grid, 2) * HALF, HALF), HALF), :].astype(jnp.int32)
    fx = lax.shift_right_logical(here, 7)
    fy = lax.bitwise_and(here, N - 1)
    fz = lax.broadcasted_iota(jnp.int32, (HALF, N), 1)
    fx = jnp.where(fx >= HALF, fx - N, fx)
    fy = jnp.where(fy >= HALF, fy - N, fy)
    fz = jnp.where(fz >= HALF, fz - N, fz)
    squares = (fx * fx + fy * fy + fz * fz).astype(F32)
    kinetic = squares * (KINETIC_COEF / float((N // 2) ** 2))
    kin[0:HALF] = kinetic
    kin[HALF:N] = kinetic

    for load in loads[2:]:
        load.wait()

    lane = lax.broadcasted_iota(jnp.int32, (slabs, N), 1)
    first = lane < HALF

    def exchange(send, recv, send_sem, recv_sem, unit):
        here_at = pl.multiple_of(my_grid * slabs, slabs)
        for peer in far_first(my_grid, n_grid, grid_far):
            there = pl.multiple_of(peer * slabs, slabs)
            pltpu.make_async_remote_copy(
                src_ref=send.at[unit, pl.ds(there, slabs)],
                dst_ref=recv.at[unit, pl.ds(here_at, slabs)],
                send_sem=send_sem.at[unit],
                recv_sem=recv_sem.at[unit],
                device_id=(my_band, peer),
                device_id_type=MESH,
            ).start()
        own = here_at
        recv[unit, pl.ds(own, slabs)] = send[unit, pl.ds(own, slabs)]

    def wait_exchange(recv, sem, unit):
        wait_bytes(recv.at[unit, pl.ds(0, N - slabs)], sem.at[unit])

    def spread(value, unit):
        real, imag = value[0:HALF], value[HALF:N]
        right = jnp.concatenate(
            [jnp.concatenate([real, -imag], axis=1), jnp.concatenate([imag, real], axis=1)], axis=0
        )
        high, low = split(right)
        send_f[unit] = lax.dot_general(
            tzi_ref[...], jnp.concatenate([high, high, low], axis=1), (((1,), (1,)), ((), ())),
            preferred_element_type=F32,
        )
        exchange(send_f, recv_f, f_send, f_recv, unit)

    def ritz_ready(which):
        wait_bytes(rs.at[which, pl.ds(0, n_band - 1)], rs_recv.at[which])
        value = rs[which, 0]
        for d in range(1, n_band):
            value = value + rs[which, d]
        coeff[which] = value
        spread(value, which)

    def place_values(unit):
        wait_exchange(recv_f, f_recv, unit)
        for j in range(chunks):
            span = slice(j * N, (j + 1) * N)
            left = recv_f[unit, 2 * j * slabs:(2 * j + 1) * slabs]
            right = recv_f[unit, (2 * j + 1) * slabs:(2 * j + 2) * slabs]
            vals[0:slabs, span] = jnp.where(first, left, pltpu.roll(right, HALF, 1))
            vals[slabs:2 * slabs, span] = jnp.where(first, pltpu.roll(left, HALF, 1), right)
        chosen = mask[...] > 0.5
        for k in range(2 * slabs):
            row = vals[k:k + 1, :]
            high = row.astype(BF16).astype(F32)
            low = row - high
            span = slice(k * LOW, (k + 1) * LOW)
            wide[span] = jnp.where(chosen, jnp.broadcast_to(high, chosen.shape), 0.0).astype(BF16)
            span = slice((2 * slabs + k) * LOW, (2 * slabs + k + 1) * LOW)
            wide[span] = jnp.where(chosen, jnp.broadcast_to(low, chosen.shape), 0.0).astype(BF16)

    def place_columns():
        placed = dot(wide[...], onehot[...]).astype(BF16)
        for part_at in range(2):
            for q in range(2):
                for s in range(slabs):
                    k = (part_at * 2 + q) * slabs + s
                    for t in range(TOP):
                        rows[
                            s * N + t * LOW:s * N + (t + 1) * LOW,
                            (part_at * 2 + q) * N:(part_at * 2 + q + 1) * N,
                        ] = placed[k * LOW:(k + 1) * LOW, t * N:(t + 1) * N]

    def right_table(which, high, low):
        return dot(
            jnp.concatenate([high, low, high], axis=1),
            jnp.concatenate([tab_ref[which], tab_ref[which], tab_ref[which + 1]], axis=0),
        )

    def left_table(which, high, low):
        return dot(
            jnp.concatenate([tab_ref[which], tab_ref[which], tab_ref[which + 1]], axis=1),
            jnp.concatenate([high, low, high], axis=0),
        )

    def turn(value, to_columns):
        count = value.shape[0 if to_columns else 1] // N
        if to_columns:
            pieces = [[value[s * N:(s + 1) * N, q * N:(q + 1) * N] for s in range(count)] for q in range(2)]
        else:
            pieces = [[value[q * N:(q + 1) * N, s * N:(s + 1) * N] for q in range(2)] for s in range(count)]
        return jnp.concatenate([jnp.concatenate(line, axis=1) for line in pieces], axis=0)

    def transform():
        def some(g, carry):
            states = []
            for h in range(SIDE):
                at = (g * SIDE + h) * PAIR
                piece = pl.ds(pl.multiple_of(at * N, N), PAIR * N)
                states.append([rows[piece, 0:2 * N], rows[piece, 2 * N:4 * N]])
            for h in range(SIDE):
                states[h] = split(turn(right_table(RIGHT_INV, *states[h]), True))
            for h in range(SIDE):
                at = (g * SIDE + h) * PAIR
                field = left_table(LEFT_INV, *states[h])
                weights = jnp.concatenate([pot_ref[at + s] for s in range(PAIR)], axis=1)
                states[h] = split(field * jnp.concatenate([weights, weights], axis=0))
            for h in range(SIDE):
                states[h] = split(turn(left_table(LEFT_FWD, *states[h]), False))
            for h in range(SIDE):
                at = (g * SIDE + h) * PAIR
                both = split(right_table(RIGHT_FWD, *states[h]))
                for p in range(2):
                    for q in range(2):
                        for s in range(PAIR):
                            for t in range(TOP):
                                read[
                                    pl.ds(pl.multiple_of((q * slabs + at + s) * LOW, LOW), LOW),
                                    (p * TOP + t) * N:(p * TOP + t + 1) * N,
                                ] = both[p][s * N + t * LOW:s * N + (t + 1) * LOW, q * N:(q + 1) * N]
            return carry

        lax.fori_loop(0, slabs // (SIDE * PAIR), some, 0)

    def read_columns(unit):
        picked = dot(read[...], jnp.concatenate([onehot_t[...], onehot_t[...]], axis=0))
        for k in range(2 * slabs):
            vals[k:k + 1, :] = jnp.sum(
                picked[k * LOW:(k + 1) * LOW] * mask[...], axis=0, keepdims=True
            )
        for j in range(chunks):
            span = slice(j * N, (j + 1) * N)
            real = vals[0:slabs, span]
            imag = vals[slabs:2 * slabs, span]
            send_b[unit, 2 * j * slabs:(2 * j + 1) * slabs] = jnp.where(
                first, real, pltpu.roll(imag, HALF, 1)
            )
            send_b[unit, (2 * j + 1) * slabs:(2 * j + 2) * slabs] = jnp.where(
                first, pltpu.roll(real, HALF, 1), imag
            )

    def plane_start(unit):
        place_values(unit)
        place_columns()
        transform()

    def plane_end(unit):
        read_columns(unit)
        exchange(send_b, recv_b, b_send, b_recv, unit)

    def plane(unit):
        plane_start(unit)
        plane_end(unit)

    def finish(unit, which):
        wait_exchange(recv_b, b_recv, unit)
        turned = recv_b[unit].T
        real, imag = turned[0:HALF], turned[HALF:N]
        left = jnp.concatenate(
            [jnp.concatenate([real, imag], axis=1), jnp.concatenate([imag, -real], axis=1)], axis=0
        )
        high, low = split(left)
        value = dot(jnp.concatenate([high, high, low], axis=1), tzf_ref[...])
        return value + kin[...] * coeff[which]

    def residual(unit):
        which = unit
        image = finish(unit, which)
        value = (image - ritz_val_ref[which] * coeff[which]) / (1.0 + kin[...])
        coeff[which] = value
        spread(value, unit + 2)
        gath[which, my_band] = value
        pltpu.make_async_copy(gath.at[which, my_band], resid_out.at[which], out_sems.at[which]).start()


    def gather_copy(which, block, owner, sems):
        return pltpu.make_async_remote_copy(
            src_ref=gath.at[which, block],
            dst_ref=gath.at[which, block],
            send_sem=g_send.at[which, sems],
            recv_sem=g_recv.at[which, sems],
            device_id=(owner, my_grid),
            device_id_type=MESH,
        )

    ring = n_band // 2
    across = flip(my_band, ring)

    def gather_own(which):
        gather_copy(which, my_band, across, 0).start()
        for offset in range(ring - 1, 0, -1):
            gather_copy(which, my_band, flip(my_band, offset), 1).start()

    def gather_across(which):
        wait_bytes(gath.at[which, 0], g_recv.at[which, 0])
        for offset in range(ring - 1, 0, -1):
            gather_copy(which, across, flip(my_band, offset), 2).start()

    def send_products():
        for which in range(2):
            for sems in (1, 2):
                wait_bytes(gath.at[which, pl.ds(0, ring - 1)], g_recv.at[which, sems])
        lines = []
        for which in range(2):
            for owner in range(n_band):
                there = gath[which, owner]
                for i in range(n_sub):
                    lines.append(jnp.sum(basis_ref[i] * there, axis=0, keepdims=True))
        high, low = split(jnp.concatenate(lines, axis=0))
        every = dot(jnp.concatenate([high, low], axis=1), jnp.ones((2 * N, N), BF16))
        lanes = lax.broadcasted_iota(jnp.int32, (n_sub, N), 1)
        total_sum = jnp.zeros((n_sub, N), F32)
        for which in range(2):
            for owner in range(n_band):
                at = (which * n_band + owner) * n_sub
                total_sum = jnp.where(lanes == 2 * owner + which, every[at:at + n_sub], total_sum)
        psend[...] = total_sum
        precv[my_grid] = total_sum

        for peer in far_first(my_grid, n_grid, grid_far):
            pltpu.make_async_remote_copy(
                src_ref=psend,
                dst_ref=precv.at[my_grid],
                send_sem=p_send,
                recv_sem=p_recv,
                device_id=(my_band, peer),
                device_id_type=MESH,
            ).start()

    ritz_ready(0)
    ritz_ready(1)
    def first_planes(unit, carry):
        plane(unit)
        return carry

    lax.fori_loop(0, 2, first_planes, 0)
    residual(0)
    gather_own(0)
    gather_across(0)
    residual(1)
    gather_own(1)
    def last_planes(unit, carry):
        plane(unit)

        @pl.when(unit == 2)
        def _():
            gather_across(1)

        return carry

    lax.fori_loop(2, 4, last_planes, 0)
    send_products()
    hres_ref[0] = finish(2, 0)
    pltpu.make_async_copy(hres_ref.at[0], hres_out.at[0], out_sems.at[2]).start()
    hres_ref[1] = finish(3, 1)
    pltpu.make_async_copy(hres_ref.at[1], hres_out.at[1], out_sems.at[3]).start()
    wait_bytes(precv.at[pl.ds(0, n_grid - 1)], p_recv)
    value = precv[0]
    for d in range(1, n_grid):
        value = value + precv[d]
    inter_ref[...] = value / float(2 * N * total)
    pltpu.make_async_copy(inter_ref, inter_out, out_sems.at[4]).start()

    for which in range(2):
        wait_bytes(part.at[which, pl.ds(0, n_band - 1)], rs_send.at[which])
        wait_bytes(gath.at[which, 0], g_send.at[which, 0])
        for sems in (1, 2):
            wait_bytes(gath.at[which, pl.ds(0, ring - 1)], g_send.at[which, sems])
    for unit in range(4):
        wait_bytes(send_f.at[unit, pl.ds(0, N - slabs)], f_send.at[unit])
        wait_bytes(send_b.at[unit, pl.ds(0, N - slabs)], b_send.at[unit])
    wait_bytes(precv.at[pl.ds(0, n_grid - 1)], p_send)
    for which in range(2):
        pltpu.make_async_copy(gath.at[which, my_band], resid_out.at[which], out_sems.at[which]).wait()
        pltpu.make_async_copy(hres_ref.at[which], hres_out.at[which], out_sems.at[2 + which]).wait()
    pltpu.make_async_copy(inter_ref, inter_out, out_sems.at[4]).wait()


def hand_out(resid_in, hres_in, inter_in, resid_out, hres_out, inter_out, held, held_inter, sems):
    there = [
        pltpu.make_async_copy(inter_in, held_inter, sems.at[0, 0]),
        pltpu.make_async_copy(hres_in, held.at[0], sems.at[0, 1]),
        pltpu.make_async_copy(resid_in, held.at[1], sems.at[0, 2]),
    ]
    back = [
        pltpu.make_async_copy(held.at[0], hres_out, sems.at[1, 1]),
        pltpu.make_async_copy(held.at[1], resid_out, sems.at[1, 2]),
    ]
    for copy in there:
        copy.start()
    there[0].wait()
    inter_out[...] = held_inter[:, 0:inter_out.shape[1]]
    for k in range(2):
        there[1 + k].wait()
        back[k].start()
    for copy in back:
        copy.wait()


def per_device(n_band, n_grid, basis, rotation, ritz_values, potential, col_map):
    n_sub = basis.shape[0]
    total = col_map.shape[0]
    slabs = N // n_grid
    inverse_z, forward_z, tables = make_tables()
    in_vmem = pl.BlockSpec(memory_space=pltpu.VMEM)
    in_hbm = pl.BlockSpec(memory_space=pltpu.HBM)
    own = (2, N, N)
    wide = (4 * slabs * LOW, total)
    rows = (slabs * N, 4 * N)
    read = (2 * slabs * LOW, 2 * TOP * N)
    dma = pltpu.SemaphoreType.DMA
    resid, h_resid, inter = pl.pallas_call(
        functools.partial(kernel, n_band, n_grid, total),
        out_shape=(
            jax.ShapeDtypeStruct(own, F32),
            jax.ShapeDtypeStruct(own, F32),
            jax.ShapeDtypeStruct((n_sub, N), F32),
        ),
        in_specs=[in_hbm] * 8,
        out_specs=(in_hbm, in_hbm, in_hbm),
        scratch_shapes=[
            pltpu.VMEM((2, N, N), F32),
            pltpu.VMEM((n_sub, N), F32),
            dma((5,)),
            pltpu.VMEM((2, n_band, N, N), F32),
            pltpu.VMEM((2, n_band, N, N), F32),
            pltpu.VMEM((2, N, N), F32),
            pltpu.VMEM((N, N), F32),
            pltpu.VMEM((total, TOP * N), BF16),
            pltpu.VMEM((TOP * N, total), BF16),
            pltpu.VMEM((LOW, total), F32),
            pltpu.VMEM((N, N), F32),
            pltpu.VMEM((4, N, N), F32),
            pltpu.VMEM((4, N, N), F32),
            pltpu.VMEM((4, N, N), F32),
            pltpu.VMEM((4, N, N), F32),
            pltpu.VMEM((2 * slabs, total), F32),
            pltpu.VMEM(wide, BF16),
            pltpu.VMEM(rows, BF16),
            pltpu.VMEM(read, BF16),
            pltpu.VMEM((2, n_band, N, N), F32),
            pltpu.VMEM((n_sub, N), F32),
            pltpu.VMEM((n_grid, n_sub, N), F32),
            pltpu.VMEM((n_sub, N, N), F32),
            pltpu.SMEM((2 * n_band, n_band * n_sub), F32),
            pltpu.SMEM((2,), F32),
            pltpu.VMEM((slabs, N, N), F32),
            pltpu.VMEM((total // N, N), jnp.int32),
            pltpu.VMEM((N, 6 * N), BF16),
            pltpu.VMEM((6 * N, N), BF16),
            pltpu.VMEM((8, 2 * N, 2 * N), BF16),
            dma((11,)),
            dma((2,)), dma((2,)), dma((4,)), dma((4,)), dma((4,)), dma((4,)),
            dma((2, 3)), dma((2, 3)), dma, dma,
        ],
        compiler_params=pltpu.CompilerParams(
            collective_id=0, has_side_effects=True, vmem_limit_bytes=56 * 1024 * 1024
        ),
    )(
        basis.reshape(n_sub, N, N), rotation.T, ritz_values, potential,
        col_map.reshape(total // N, N), jnp.asarray(inverse_z), jnp.asarray(forward_z),
        jnp.asarray(tables),
    )
    resid, h_resid, inter = pl.pallas_call(
        hand_out,
        out_shape=(
            jax.ShapeDtypeStruct(own, F32),
            jax.ShapeDtypeStruct(own, F32),
            jax.ShapeDtypeStruct((n_sub, 2 * n_band), F32),
        ),
        in_specs=[in_hbm] * 3,
        out_specs=(in_hbm, in_hbm, in_vmem),
        scratch_shapes=[pltpu.VMEM((2,) + own, F32), pltpu.VMEM((n_sub, N), F32), dma((2, 3))],
        compiler_params=pltpu.CompilerParams(vmem_limit_bytes=56 * 1024 * 1024),
    )(resid, h_resid, inter)
    shape = (2, 2, HALF, N)
    return resid.reshape(shape), h_resid.reshape(shape), inter


def solution(mesh):
    placed = (P("band", None, "grid", None), P(), P("band"), P("grid", None, None), P())
    return jax.shard_map(
        functools.partial(per_device, mesh.shape["band"], mesh.shape["grid"]),
        mesh=mesh,
        in_specs=placed,
        out_specs=(P("band", None, "grid", None), P("band", None, "grid", None), P("band", None)),
        check_vma=False,
    )
```

```python
import functools

import jax
import jax.numpy as jnp
import ml_dtypes
import numpy as np
from jax import lax
from jax.experimental import pallas as pl
from jax.experimental.pallas import tpu as pltpu
from jax.sharding import PartitionSpec as P

MESH = pl.DeviceIdType.MESH
N = 128
HALF = 64
LOW = 32
TOP = N // LOW
KINETIC_COEF = 2.0
PAIR = 2
SIDE = 4
F32 = jnp.float32
BF16 = jnp.bfloat16


def angle_tables():
    index = np.arange(N)
    angles = 2.0 * np.pi * (np.outer(index, index) % N) / N
    return np.cos(angles), np.sin(angles)


def split_table(table):
    high = table.astype(ml_dtypes.bfloat16)
    low = (table - high.astype(np.float64)).astype(ml_dtypes.bfloat16)
    return np.stack([high, low])


def make_tables():
    cosine, sine = angle_tables()
    high, low = split_table(np.concatenate([cosine, sine], axis=1) / N)
    inverse_z = np.concatenate([high, low, high], axis=1)
    high, low = split_table(np.concatenate([cosine, sine], axis=0))
    forward_z = np.concatenate([high, low, high], axis=0)
    inverse = np.block([[cosine, sine], [-sine, cosine]]) / N
    forward = np.block([[cosine, -sine], [sine, cosine]])
    tables = np.concatenate(
        [split_table(inverse), split_table(inverse.T), split_table(forward), split_table(forward.T)]
    )
    return inverse_z, forward_z, tables


RIGHT_INV, LEFT_INV, RIGHT_FWD, LEFT_FWD = 0, 2, 4, 6


def grid_far(offset):
    x = offset // 4
    return (x if x < 3 else 1) + 2 * (offset // 2 % 2)


def band_far(offset):
    y = offset % 4
    return (y if y < 3 else 1) + offset // 4


def flip(index, offset):
    bit = 1
    while bit <= offset:
        if offset & bit:
            index = index + bit - 2 * bit * (index // bit % 2)
        bit *= 2
    return index


def far_first(index, count, far):
    order = sorted(range(1, count), key=lambda offset: -far(offset))
    return [flip(index, offset) for offset in order]


def split(value):
    high = value.astype(BF16)
    return high, (value - high.astype(F32)).astype(BF16)


def dot(left, right):
    return jnp.dot(left, right, preferred_element_type=F32)


def wait_bytes(view, sem):
    pltpu.make_async_copy(view, view, sem).wait()


def kernel(
    n_band, n_grid, total,
    basis_in, rot_in, ritz_val_in, pot_in, map_in, tzi_in, tzf_in, tab_in,
    resid_out, hres_out, inter_out,
    hres_ref, inter_ref, out_sems,
    part, rs, coeff, kin, onehot, onehot_t, mask, tmp,
    send_f, recv_f, send_b, recv_b,
    vals, wide, rows, read,
    gath, acc, psend, precv,
    basis_ref, rot_ref, ritz_val_ref, pot_ref, map_ref, tzi_ref, tzf_ref, tab_ref, in_sems,
    rs_send, rs_recv, f_send, f_recv, b_send, b_recv, g_send, g_recv, p_send, p_recv,
):
    slabs = N // n_grid
    chunks = total // N
    n_sub = basis_ref.shape[0]
    my_band = lax.axis_index("band")
    my_grid = lax.axis_index("grid")

    loads = [
        pltpu.make_async_copy(source, target, in_sems.at[k])
        for k, (source, target) in enumerate(
            (
                (rot_in, rot_ref),
                (basis_in, basis_ref),
                (map_in, map_ref),
                (tzi_in, tzi_ref),
                (tab_in, tab_ref),
                (pot_in, pot_ref),
                (tzf_in, tzf_ref),
                (ritz_val_in, ritz_val_ref),
            )
        )
    ]
    barrier = pltpu.get_barrier_semaphore()

    def greet_band(step, carry):
        peer = lax.rem(my_band + step, n_band)
        pl.semaphore_signal(barrier, inc=1, device_id=(peer, my_grid), device_id_type=MESH)
        return carry

    def greet_grid(step, carry):
        peer = lax.rem(my_grid + step, n_grid)
        pl.semaphore_signal(barrier, inc=1, device_id=(my_band, peer), device_id_type=MESH)
        return carry

    lax.fori_loop(1, n_band, greet_band, 0)
    lax.fori_loop(1, n_grid, greet_grid, 0)
    for load in loads:
        load.start()

    def partial_of(owner, which):
        column = owner * 2 + which
        row = my_band * n_sub
        value = rot_ref[column, row] * basis_ref[0]
        for i in range(1, n_sub):
            value = value + rot_ref[column, row + i] * basis_ref[i]
        return value

    loads[0].wait()
    loads[1].wait()
    started = False
    for which in range(2):
        for owner in far_first(my_band, n_band, band_far):
            part[which, owner] = partial_of(owner, which)
            if not started:
                pl.semaphore_wait(barrier, n_band - 1 + n_grid - 1)
                started = True
            pltpu.make_async_remote_copy(
                src_ref=part.at[which, owner],
                dst_ref=rs.at[which, my_band],
                send_sem=rs_send.at[which],
                recv_sem=rs_recv.at[which],
                device_id=(owner, my_grid),
                device_id_type=MESH,
            ).start()
        rs[which, my_band] = partial_of(my_band, which)
    loads[2].wait()

    lane_c = lax.broadcasted_iota(jnp.int32, (TOP * N, N), 0)
    lane_r = lax.broadcasted_iota(jnp.int32, (LOW, N), 0)
    for j in range(chunks):
        span = slice(j * N, (j + 1) * N)
        pos = map_ref[j:j + 1, :]
        x = lax.shift_right_logical(pos, 7)
        y = lax.bitwise_and(pos, N - 1)
        high = lax.shift_right_logical(x, 5) * N + y
        hit = jnp.where(lane_c == jnp.broadcast_to(high, lane_c.shape), 1.0, 0.0)
        onehot_t[:, span] = hit.astype(BF16)
        for t in range(TOP):
            onehot[span, t * N:(t + 1) * N] = hit[t * N:(t + 1) * N].T.astype(BF16)
        low = jnp.broadcast_to(lax.bitwise_and(x, LOW - 1), lane_r.shape)
        mask[:, span] = jnp.where(lane_r == low, 1.0, 0.0)

    mine = map_ref[pl.ds(my_grid // 2, 1), :].astype(F32)
    tmp[...] = jnp.broadcast_to(mine, (N, N)).T
    here = tmp[pl.ds(pl.multiple_of(lax.rem(my_grid, 2) * HALF, HALF), HALF), :].astype(jnp.int32)
    fx = lax.shift_right_logical(here, 7)
    fy = lax.bitwise_and(here, N - 1)
    fz = lax.broadcasted_iota(jnp.int32, (HALF, N), 1)
    fx = jnp.where(fx >= HALF, fx - N, fx)
    fy = jnp.where(fy >= HALF, fy - N, fy)
    fz = jnp.where(fz >= HALF, fz - N, fz)
    squares = (fx * fx + fy * fy + fz * fz).astype(F32)
    kinetic = squares * (KINETIC_COEF / float((N // 2) ** 2))
    kin[0:HALF] = kinetic
    kin[HALF:N] = kinetic

    for load in loads[3:]:
        load.wait()

    lane = lax.broadcasted_iota(jnp.int32, (slabs, N), 1)
    first = lane < HALF

    def exchange(send, recv, send_sem, recv_sem, unit):
        here_at = pl.multiple_of(my_grid * slabs, slabs)
        for peer in far_first(my_grid, n_grid, grid_far):
            there = pl.multiple_of(peer * slabs, slabs)
            pltpu.make_async_remote_copy(
                src_ref=send.at[unit, pl.ds(there, slabs)],
                dst_ref=recv.at[unit, pl.ds(here_at, slabs)],
                send_sem=send_sem.at[unit],
                recv_sem=recv_sem.at[unit],
                device_id=(my_band, peer),
                device_id_type=MESH,
            ).start()
        own = here_at
        recv[unit, pl.ds(own, slabs)] = send[unit, pl.ds(own, slabs)]

    def wait_exchange(recv, sem, unit):
        wait_bytes(recv.at[unit, pl.ds(0, N - slabs)], sem.at[unit])

    def spread(value, unit):
        real, imag = value[0:HALF], value[HALF:N]
        right = jnp.concatenate(
            [jnp.concatenate([real, -imag], axis=1), jnp.concatenate([imag, real], axis=1)], axis=0
        )
        high, low = split(right)
        send_f[unit] = lax.dot_general(
            tzi_ref[...], jnp.concatenate([high, high, low], axis=1), (((1,), (1,)), ((), ())),
            preferred_element_type=F32,
        )
        exchange(send_f, recv_f, f_send, f_recv, unit)

    def ritz_ready(which):
        wait_bytes(rs.at[which, pl.ds(0, n_band - 1)], rs_recv.at[which])
        value = rs[which, 0]
        for d in range(1, n_band):
            value = value + rs[which, d]
        coeff[which] = value
        spread(value, which)

    def place_values(unit):
        wait_exchange(recv_f, f_recv, unit)
        for j in range(chunks):
            span = slice(j * N, (j + 1) * N)
            left = recv_f[unit, 2 * j * slabs:(2 * j + 1) * slabs]
            right = recv_f[unit, (2 * j + 1) * slabs:(2 * j + 2) * slabs]
            vals[0:slabs, span] = jnp.where(first, left, pltpu.roll(right, HALF, 1))
            vals[slabs:2 * slabs, span] = jnp.where(first, pltpu.roll(left, HALF, 1), right)
        chosen = mask[...] > 0.5
        for k in range(2 * slabs):
            row = vals[k:k + 1, :]
            high = row.astype(BF16).astype(F32)
            low = row - high
            span = slice(k * LOW, (k + 1) * LOW)
            wide[span] = jnp.where(chosen, jnp.broadcast_to(high, chosen.shape), 0.0).astype(BF16)
            span = slice((2 * slabs + k) * LOW, (2 * slabs + k + 1) * LOW)
            wide[span] = jnp.where(chosen, jnp.broadcast_to(low, chosen.shape), 0.0).astype(BF16)

    def place_columns():
        placed = dot(wide[...], onehot[...]).astype(BF16)
        for part_at in range(2):
            for q in range(2):
                for s in range(slabs):
                    k = (part_at * 2 + q) * slabs + s
                    for t in range(TOP):
                        rows[
                            s * N + t * LOW:s * N + (t + 1) * LOW,
                            (part_at * 2 + q) * N:(part_at * 2 + q + 1) * N,
                        ] = placed[k * LOW:(k + 1) * LOW, t * N:(t + 1) * N]

    def right_table(which, high, low):
        return dot(
            jnp.concatenate([high, low, high], axis=1),
            jnp.concatenate([tab_ref[which], tab_ref[which], tab_ref[which + 1]], axis=0),
        )

    def left_table(which, high, low):
        return dot(
            jnp.concatenate([tab_ref[which], tab_ref[which], tab_ref[which + 1]], axis=1),
            jnp.concatenate([high, low, high], axis=0),
        )

    def turn(value, to_columns):
        count = value.shape[0 if to_columns else 1] // N
        if to_columns:
            pieces = [[value[s * N:(s + 1) * N, q * N:(q + 1) * N] for s in range(count)] for q in range(2)]
        else:
            pieces = [[value[q * N:(q + 1) * N, s * N:(s + 1) * N] for q in range(2)] for s in range(count)]
        return jnp.concatenate([jnp.concatenate(line, axis=1) for line in pieces], axis=0)

    def transform():
        def some(g, carry):
            states = []
            for h in range(SIDE):
                at = (g * SIDE + h) * PAIR
                piece = pl.ds(pl.multiple_of(at * N, N), PAIR * N)
                states.append([rows[piece, 0:2 * N], rows[piece, 2 * N:4 * N]])
            for h in range(SIDE):
                states[h] = split(turn(right_table(RIGHT_INV, *states[h]), True))
            for h in range(SIDE):
                at = (g * SIDE + h) * PAIR
                field = left_table(LEFT_INV, *states[h])
                weights = jnp.concatenate([pot_ref[at + s] for s in range(PAIR)], axis=1)
                states[h] = split(field * jnp.concatenate([weights, weights], axis=0))
            for h in range(SIDE):
                states[h] = split(turn(left_table(LEFT_FWD, *states[h]), False))
            for h in range(SIDE):
                at = (g * SIDE + h) * PAIR
                both = split(right_table(RIGHT_FWD, *states[h]))
                for p in range(2):
                    for q in range(2):
                        for s in range(PAIR):
                            for t in range(TOP):
                                read[
                                    pl.ds(pl.multiple_of((q * slabs + at + s) * LOW, LOW), LOW),
                                    (p * TOP + t) * N:(p * TOP + t + 1) * N,
                                ] = both[p][s * N + t * LOW:s * N + (t + 1) * LOW, q * N:(q + 1) * N]
            return carry

        lax.fori_loop(0, slabs // (SIDE * PAIR), some, 0)

    def read_columns(unit):
        picked = dot(read[...], jnp.concatenate([onehot_t[...], onehot_t[...]], axis=0))
        for k in range(2 * slabs):
            vals[k:k + 1, :] = jnp.sum(
                picked[k * LOW:(k + 1) * LOW] * mask[...], axis=0, keepdims=True
            )
        for j in range(chunks):
            span = slice(j * N, (j + 1) * N)
            real = vals[0:slabs, span]
            imag = vals[slabs:2 * slabs, span]
            send_b[unit, 2 * j * slabs:(2 * j + 1) * slabs] = jnp.where(
                first, real, pltpu.roll(imag, HALF, 1)
            )
            send_b[unit, (2 * j + 1) * slabs:(2 * j + 2) * slabs] = jnp.where(
                first, pltpu.roll(real, HALF, 1), imag
            )

    def plane_start(unit):
        place_values(unit)
        place_columns()
        transform()

    def plane_end(unit):
        read_columns(unit)
        exchange(send_b, recv_b, b_send, b_recv, unit)

    def plane(unit):
        plane_start(unit)
        plane_end(unit)

    def finish(unit, which):
        wait_exchange(recv_b, b_recv, unit)
        turned = recv_b[unit].T
        real, imag = turned[0:HALF], turned[HALF:N]
        left = jnp.concatenate(
            [jnp.concatenate([real, imag], axis=1), jnp.concatenate([imag, -real], axis=1)], axis=0
        )
        high, low = split(left)
        value = dot(jnp.concatenate([high, high, low], axis=1), tzf_ref[...])
        return value + kin[...] * coeff[which]

    def residual(unit):
        which = unit
        image = finish(unit, which)
        value = (image - ritz_val_ref[which] * coeff[which]) / (1.0 + kin[...])
        coeff[which] = value
        spread(value, unit + 2)
        gath[which, my_band] = value
        pltpu.make_async_copy(gath.at[which, my_band], resid_out.at[which], out_sems.at[which]).start()


    def gather_copy(which, block, owner, sems):
        return pltpu.make_async_remote_copy(
            src_ref=gath.at[which, block],
            dst_ref=gath.at[which, block],
            send_sem=g_send.at[which, sems],
            recv_sem=g_recv.at[which, sems],
            device_id=(owner, my_grid),
            device_id_type=MESH,
        )

    ring = n_band // 2
    across = flip(my_band, ring)

    def gather_own(which):
        gather_copy(which, my_band, across, 0).start()
        for offset in range(ring - 1, 0, -1):
            gather_copy(which, my_band, flip(my_band, offset), 1).start()

    def gather_across(which):
        wait_bytes(gath.at[which, 0], g_recv.at[which, 0])
        for offset in range(ring - 1, 0, -1):
            gather_copy(which, across, flip(my_band, offset), 2).start()

    def products(which):
        for sems in (1, 2):
            wait_bytes(gath.at[which, pl.ds(0, ring - 1)], g_recv.at[which, sems])

        lines = []
        for owner in range(n_band):
            there = gath[which, owner]
            for i in range(n_sub):
                lines.append(jnp.sum(basis_ref[i] * there, axis=0, keepdims=True))
        high, low = split(jnp.concatenate(lines, axis=0))
        every = dot(jnp.concatenate([high, low], axis=1), jnp.ones((2 * N, N), BF16))
        lanes = lax.broadcasted_iota(jnp.int32, (n_sub, N), 1)
        found = jnp.zeros((n_sub, N), F32)
        for owner in range(n_band):
            found = jnp.where(lanes == 2 * owner + which, every[owner * n_sub:(owner + 1) * n_sub], found)
        acc[which] = found

    def send_products():
        total_sum = acc[0] + acc[1]
        psend[...] = total_sum
        precv[my_grid] = total_sum

        for peer in far_first(my_grid, n_grid, grid_far):
            pltpu.make_async_remote_copy(
                src_ref=psend,
                dst_ref=precv.at[my_grid],
                send_sem=p_send,
                recv_sem=p_recv,
                device_id=(my_band, peer),
                device_id_type=MESH,
            ).start()

    ritz_ready(0)
    ritz_ready(1)
    def first_planes(unit, carry):
        plane(unit)
        return carry

    lax.fori_loop(0, 2, first_planes, 0)
    residual(0)
    gather_own(0)
    residual(1)
    gather_own(1)
    gather_across(0)
    def last_planes(unit, carry):
        plane(unit)

        @pl.when(unit == 2)
        def _():
            gather_across(1)

        return carry

    lax.fori_loop(2, 4, last_planes, 0)
    products(0)
    products(1)
    send_products()
    hres_ref[0] = finish(2, 0)
    pltpu.make_async_copy(hres_ref.at[0], hres_out.at[0], out_sems.at[2]).start()
    hres_ref[1] = finish(3, 1)
    pltpu.make_async_copy(hres_ref.at[1], hres_out.at[1], out_sems.at[3]).start()
    wait_bytes(precv.at[pl.ds(0, n_grid - 1)], p_recv)
    value = precv[0]
    for d in range(1, n_grid):
        value = value + precv[d]
    inter_ref[...] = value / float(2 * N * total)
    pltpu.make_async_copy(inter_ref, inter_out, out_sems.at[4]).start()

    for which in range(2):
        wait_bytes(part.at[which, pl.ds(0, n_band - 1)], rs_send.at[which])
        wait_bytes(gath.at[which, 0], g_send.at[which, 0])
        for sems in (1, 2):
            wait_bytes(gath.at[which, pl.ds(0, ring - 1)], g_send.at[which, sems])
    for unit in range(4):
        wait_bytes(send_f.at[unit, pl.ds(0, N - slabs)], f_send.at[unit])
        wait_bytes(send_b.at[unit, pl.ds(0, N - slabs)], b_send.at[unit])
    wait_bytes(precv.at[pl.ds(0, n_grid - 1)], p_send)
    for which in range(2):
        pltpu.make_async_copy(gath.at[which, my_band], resid_out.at[which], out_sems.at[which]).wait()
        pltpu.make_async_copy(hres_ref.at[which], hres_out.at[which], out_sems.at[2 + which]).wait()
    pltpu.make_async_copy(inter_ref, inter_out, out_sems.at[4]).wait()


def hand_out(resid_in, hres_in, inter_in, resid_out, hres_out, inter_out, held, held_inter, sems):
    there = [
        pltpu.make_async_copy(inter_in, held_inter, sems.at[0, 0]),
        pltpu.make_async_copy(hres_in, held.at[0], sems.at[0, 1]),
        pltpu.make_async_copy(resid_in, held.at[1], sems.at[0, 2]),
    ]
    back = [
        pltpu.make_async_copy(held.at[0], hres_out, sems.at[1, 1]),
        pltpu.make_async_copy(held.at[1], resid_out, sems.at[1, 2]),
    ]
    for copy in there:
        copy.start()
    there[0].wait()
    inter_out[...] = held_inter[:, 0:inter_out.shape[1]]
    for k in range(2):
        there[1 + k].wait()
        back[k].start()
    for copy in back:
        copy.wait()


def per_device(n_band, n_grid, basis, rotation, ritz_values, potential, col_map):
    n_sub = basis.shape[0]
    total = col_map.shape[0]
    slabs = N // n_grid
    inverse_z, forward_z, tables = make_tables()
    in_vmem = pl.BlockSpec(memory_space=pltpu.VMEM)
    in_hbm = pl.BlockSpec(memory_space=pltpu.HBM)
    own = (2, N, N)
    wide = (4 * slabs * LOW, total)
    rows = (slabs * N, 4 * N)
    read = (2 * slabs * LOW, 2 * TOP * N)
    dma = pltpu.SemaphoreType.DMA
    resid, h_resid, inter = pl.pallas_call(
        functools.partial(kernel, n_band, n_grid, total),
        out_shape=(
            jax.ShapeDtypeStruct(own, F32),
            jax.ShapeDtypeStruct(own, F32),
            jax.ShapeDtypeStruct((n_sub, N), F32),
        ),
        in_specs=[in_hbm] * 8,
        out_specs=(in_hbm, in_hbm, in_hbm),
        scratch_shapes=[
            pltpu.VMEM((2, N, N), F32),
            pltpu.VMEM((n_sub, N), F32),
            dma((5,)),
            pltpu.VMEM((2, n_band, N, N), F32),
            pltpu.VMEM((2, n_band, N, N), F32),
            pltpu.VMEM((2, N, N), F32),
            pltpu.VMEM((N, N), F32),
            pltpu.VMEM((total, TOP * N), BF16),
            pltpu.VMEM((TOP * N, total), BF16),
            pltpu.VMEM((LOW, total), F32),
            pltpu.VMEM((N, N), F32),
            pltpu.VMEM((4, N, N), F32),
            pltpu.VMEM((4, N, N), F32),
            pltpu.VMEM((4, N, N), F32),
            pltpu.VMEM((4, N, N), F32),
            pltpu.VMEM((2 * slabs, total), F32),
            pltpu.VMEM(wide, BF16),
            pltpu.VMEM(rows, BF16),
            pltpu.VMEM(read, BF16),
            pltpu.VMEM((2, n_band, N, N), F32),
            pltpu.VMEM((2, n_sub, N), F32),
            pltpu.VMEM((n_sub, N), F32),
            pltpu.VMEM((n_grid, n_sub, N), F32),
            pltpu.VMEM((n_sub, N, N), F32),
            pltpu.SMEM((2 * n_band, n_band * n_sub), F32),
            pltpu.SMEM((2,), F32),
            pltpu.VMEM((slabs, N, N), F32),
            pltpu.VMEM((total // N, N), jnp.int32),
            pltpu.VMEM((N, 6 * N), BF16),
            pltpu.VMEM((6 * N, N), BF16),
            pltpu.VMEM((8, 2 * N, 2 * N), BF16),
            dma((8,)),
            dma((2,)), dma((2,)), dma((4,)), dma((4,)), dma((4,)), dma((4,)),
            dma((2, 3)), dma((2, 3)), dma, dma,
        ],
        compiler_params=pltpu.CompilerParams(
            collective_id=0, has_side_effects=True, vmem_limit_bytes=56 * 1024 * 1024
        ),
    )(
        basis.reshape(n_sub, N, N), rotation.T, ritz_values, potential,
        col_map.reshape(total // N, N), jnp.asarray(inverse_z), jnp.asarray(forward_z),
        jnp.asarray(tables),
    )
    resid, h_resid, inter = pl.pallas_call(
        hand_out,
        out_shape=(
            jax.ShapeDtypeStruct(own, F32),
            jax.ShapeDtypeStruct(own, F32),
            jax.ShapeDtypeStruct((n_sub, 2 * n_band), F32),
        ),
        in_specs=[in_hbm] * 3,
        out_specs=(in_hbm, in_hbm, in_vmem),
        scratch_shapes=[pltpu.VMEM((2,) + own, F32), pltpu.VMEM((n_sub, N), F32), dma((2, 3))],
        compiler_params=pltpu.CompilerParams(vmem_limit_bytes=56 * 1024 * 1024),
    )(resid, h_resid, inter)
    shape = (2, 2, HALF, N)
    return resid.reshape(shape), h_resid.reshape(shape), inter


def solution(mesh):
    placed = (P("band", None, "grid", None), P(), P("band"), P("grid", None, None), P())
    return jax.shard_map(
        functools.partial(per_device, mesh.shape["band"], mesh.shape["grid"]),
        mesh=mesh,
        in_specs=placed,
        out_specs=(P("band", None, "grid", None), P("band", None, "grid", None), P("band", None)),
        check_vma=False,
    )
```
